256 devices in a mesh: mod: 8 (over z), dp: 32 (over x, y, core).
Axes of the slice: x: 4, y: 4, z: 8, core: 2. Of those that a mesh axis runs over, the one named last changes fastest.
Arguments:
- train_grads: float32 [4096, 128, 512], P('dp', 'mod'), may hold values from -50 to 50
- queries: float32 [128, 128, 512], P('dp', 'mod'), may hold values from -6 to 6
- damping: float32 [128], P('mod'), may hold values from 0.05 to 0.5
Outputs:
- scores: float32 [4096, 128], P('dp', 'mod')
The draws below stay inside these ranges and needn't reach their ends.
All inputs are finite; a program needn't handle non-finite values.
Results may differ from the reference program's by a relative error of at most 0.012.
Values sent between devices are 32-bit elements; how exact they have to be, the bound alone decides.
A program may use at most 128 MiB of HBM per device.

```python
import math
import jax
import jax.numpy as jnp
from jax import lax

PROJ_DIM = 512
NEWTON_STEPS = 8
MODULES = 128
ROWS = 4096
QUERIES = 128


def draw_train_grads(key, part):
    keys = jax.random.split(key, 3)
    spread = 1.1512925
    row_scale = jnp.exp(jax.random.uniform(keys[0], (ROWS, 1, 1), jnp.float32, -spread, spread))
    col_scale = jnp.exp(jax.random.uniform(keys[1], (1, MODULES, PROJ_DIM), jnp.float32, -spread, spread))
    base = jnp.clip(jax.random.normal(keys[2], (ROWS, MODULES, PROJ_DIM), jnp.float32), -4.0, 4.0)
    return base * row_scale * col_scale


def steps_of(rng, extent, cuts, low, high):
    factor_of, own = 1.0, jax.random.fold_in(rng, 6)
    for axis_at, shards_of in cuts:
        heights = jnp.exp(jax.random.uniform(jax.random.fold_in(own, axis_at), (shards_of,), jnp.float32, low / len(cuts), high / len(cuts)))
        factor_of = factor_of * jnp.repeat(heights, extent[axis_at] // shards_of).reshape([-1 if axis == axis_at else 1 for axis in range(len(extent))])
    return factor_of


def bell_draw(key, dims, deviation, bound, shards=(), kind=jnp.bfloat16):
    loudness = steps_of(key, dims, shards, -0.22, 0.18) if shards else 1.0
    drawn = jax.random.normal(key, dims, jnp.float32) * deviation * loudness
    return jnp.minimum(jnp.maximum(drawn, -bound), bound).astype(kind)


def setup_inputs(seed: int = 0) -> dict:
    streams_of = jax.random.split(jax.random.key(seed), 4)
    return {
        "train_grads": draw_train_grads(jax.random.fold_in(streams_of[3], 71), 0),
        "queries": bell_draw(streams_of[1], (QUERIES, MODULES, PROJ_DIM), 1.0, 6.0, ((0, 32), (1, 8)), jnp.float32),
        "damping": jnp.clip(jnp.exp(math.log(0.5) - 2.3025851 * jax.random.uniform(streams_of[2], (MODULES,), jnp.float32) ** steps_of(streams_of[2], (MODULES,), ((0, 8),), -0.2, 0.2)), 0.05, 0.5),
    }


epsilon = 1e-06

def module_term(grads_module, queries_module, damp_value):
    highest = lax.Precision.HIGHEST
    fisher = lax.dot_general(grads_module, grads_module, (((0,), (0,)), ((), ())), precision=highest, preferred_element_type=jnp.float32) / ROWS
    trace_all = jnp.trace(fisher)
    damp_shift = damp_value * trace_all / PROJ_DIM
    identity_mat = jnp.eye(PROJ_DIM, dtype=jnp.float32)
    system = fisher + damp_shift * identity_mat
    frob_norm = jnp.sqrt(jnp.sum(system * system) + epsilon)
    inverse = identity_mat / frob_norm
    for iteration in range(NEWTON_STEPS):
        product = jnp.dot(jnp.dot(inverse, system, precision=highest, preferred_element_type=jnp.float32), inverse, precision=highest, preferred_element_type=jnp.float32)
        inverse = 2.0 * inverse - product
    conditioned = jnp.dot(queries_module, inverse, precision=highest, preferred_element_type=jnp.float32)
    return lax.dot_general(grads_module, conditioned, (((1,), (1,)), ((), ())), precision=highest, preferred_element_type=jnp.float32)

def reference(train_grads, queries, damping):

    def add_module(module, running):
        grads_module = lax.dynamic_index_in_dim(train_grads, module, 1, keepdims=False)
        queries_module = lax.dynamic_index_in_dim(queries, module, 1, keepdims=False)
        damp_value = lax.dynamic_index_in_dim(damping, module, 0, keepdims=False)
        return running + module_term(grads_module, queries_module, damp_value)
    running = lax.fori_loop(0, MODULES, add_module, jnp.zeros((ROWS, QUERIES), jnp.float32))
    return running / math.sqrt(MODULES * PROJ_DIM)
```

```python
import functools
import math

import jax
import jax.numpy as jnp
from jax import lax
from jax.experimental import pallas as pl
from jax.experimental.pallas import tpu as pltpu
from jax.sharding import PartitionSpec as P

NEWTON_STEPS = 8
EPSILON = 1e-06

SIDE = 4
CHIPS = SIDE * SIDE
DEPTH = 8
WIDTH = 512
ROWS = 128
LANES = 128
TRI = 4 * LANES + 8
TOP = 264
HALF_Q = 64
BF16 = jnp.bfloat16
F32 = jnp.float32

RAW = 0
QRY = RAW + 16
R1 = QRY + 16
R2 = R1 + 4
R3 = R2 + 8
R4 = R3 + 2
EXC = R4 + 4
SEC = EXC + 1
FST = SEC + 4
PAR = FST + 16
ZED = PAR + 16
COPIES = ZED + 8


def split(value):
    high = value.astype(BF16)
    return high, (value - high.astype(F32)).astype(BF16)


def dot(a, b):
    return jnp.dot(a, b, preferred_element_type=F32)


def dot_t(a, b):
    return lax.dot_general(a, b, (((1,), (1,)), ((), ())), preferred_element_type=F32)


def wrap(i):
    return lax.rem(i + 2 * SIDE, SIDE)


def kernel(
    total_rows,
    scale,
    x_hbm,
    q_hbm,
    damp_ref,
    out_ref,
    x,
    q_in,
    stage,
    rx,
    qstage,
    qrx,
    part,
    r1,
    r2,
    r3,
    r4,
    half,
    p_ref,
    cond,
    g_hi,
    g_lo,
    acc,
    zout,
    zin,
    in_sem,
    send,
    recv,
):
    z = lax.axis_index("mod")
    dp = lax.axis_index("dp")
    core = lax.rem(dp, 2)
    chip = lax.div(dp, 2)
    cx = lax.div(chip, SIDE)
    cy = lax.rem(chip, SIDE)
    fst = cx * (1 - core) + cy * core
    snd = cy * (1 - core) + cx * core

    def chip_at(p, q, c=core):
        return (p * (1 - c) + q * c) * SIDE + q * (1 - c) + p * c

    def dev(p, q):
        return (z, chip_at(wrap(p), wrap(q)) * 2 + core)

    partner = (z, chip * 2 + 1 - core)

    def copy(src, dst, place, device):
        return pltpu.make_async_remote_copy(
            src_ref=src,
            dst_ref=dst,
            send_sem=send.at[place],
            recv_sem=recv.at[place],
            device_id=device,
            device_id_type=pl.DeviceIdType.MESH,
        )

    loads = []
    for lb in range(4):
        cols = pl.ds(lb * LANES, LANES)
        loads.append(pltpu.make_async_copy(x_hbm.at[:, cols], x.at[lb], in_sem.at[lb]))
        loads.append(pltpu.make_async_copy(q_hbm.at[:, cols], q_in.at[lb], in_sem.at[4 + lb]))
    for load in loads:
        load.start()

    barrier = pltpu.get_barrier_semaphore()

    def greet_chip(i, carry):
        there = lax.rem(chip + i, CHIPS)
        pl.semaphore_signal(
            barrier, inc=1, device_id=(z, there * 2 + core), device_id_type=pl.DeviceIdType.MESH
        )
        return carry

    lax.fori_loop(1, CHIPS, greet_chip, 0)

    def greet_layer(i, carry):
        pl.semaphore_signal(
            barrier, inc=1, device_id=(lax.rem(z + i, DEPTH), dp), device_id_type=pl.DeviceIdType.MESH
        )
        return carry

    lax.fori_loop(1, DEPTH, greet_layer, 0)
    pl.semaphore_signal(barrier, inc=1, device_id=partner, device_id_type=pl.DeviceIdType.MESH)
    for load in loads:
        load.wait()
    pl.semaphore_wait(barrier, CHIPS - 1 + DEPTH - 1 + 1)

    def second_of(b):
        return lax.rem(2 + 3 * b + lax.div(b, 2) * (3 - 2 * lax.rem(b, 2)), SIDE)

    def order(k):
        group = lax.div(k, 4)
        i = lax.rem(k, 4)
        odd = lax.rem(i, 2)
        is0 = lax.div(3 - group, 3)
        is1 = lax.rem(group, 2) * (1 - lax.div(group, 3))
        is3 = lax.div(group, 3)
        first = is0 * 2 + (1 - is0 - is3) * (1 + 2 * odd)
        b = i + is1 * (1 - 2 * odd)
        return first, b

    def module_of(k, c):
        first, b = order(k)
        p = cx * (1 - c) + cy * c
        q = cy * (1 - c) + cx * c
        return chip_at(lax.rem(p + first, SIDE), lax.rem(q + second_of(b), SIDE), c)

    def send_raw(k, carry):
        j = module_of(k, 1 - core)
        for lb in range(4):
            cols = pl.ds(lb * LANES, LANES)
            stage[j, :, cols] = x[lb, pl.ds(j, ROWS, stride=CHIPS), :]
        copy(stage.at[j], rx.at[j], RAW + k, partner).start()
        return carry

    lax.fori_loop(0, CHIPS, send_raw, 0)

    def stage_query(j, carry):
        for lb in range(4):
            cols = pl.ds(lb * LANES, LANES)
            rows = q_in[lb, pl.ds(j, 4, stride=CHIPS), :]
            qstage[j, :, cols] = jnp.concatenate([rows, rows], axis=0)
        return carry

    lax.fori_loop(0, CHIPS, stage_query, 0)

    def send_query(i, carry):
        there = lax.rem(chip + i, CHIPS)
        copy(qstage.at[there], qrx.at[chip], QRY + i, (z, there * 2 + core)).start()
        return carry

    lax.fori_loop(1, CHIPS, send_query, 0)
    qrx[chip] = qstage[chip]

    row_of = lax.broadcasted_iota(jnp.int32, (LANES, LANES), 0)
    col_of = lax.broadcasted_iota(jnp.int32, (LANES, LANES), 1)
    upper = row_of <= col_of
    eye = row_of == col_of

    def gram(k):
        j = module_of(k, core)
        copy(stage.at[j], rx.at[j], RAW + k, partner).wait_recv()
        blocks, highs, lows = [], [], []
        for lb in range(4):
            cols = pl.ds(pl.multiple_of(lax.rem(lb + core, 4) * LANES, LANES), LANES)
            block = jnp.concatenate([stage[j, :, cols], rx[j, :, cols]], axis=0)
            high, low = split(block)
            g_hi[j, :, cols] = high[:ROWS]
            g_lo[j, :, cols] = low[:ROWS]
            blocks.append(block)
            highs.append(high)
            lows.append(low)
        left = jnp.concatenate([blocks[0].T, blocks[2].T], axis=0)
        left_hi, left_lo = split(left)
        right_hi = jnp.concatenate(highs, axis=1)
        right_lo = jnp.concatenate(lows, axis=1)
        prod = dot(left_hi, right_hi) + (dot(left_hi, right_lo) + dot(left_lo, right_hi))
        first, second = prod[:LANES], prod[LANES:]
        one, two = first[:, :LANES], second[:, 2 * LANES : 3 * LANES]
        diagonal = jnp.sum(jnp.where(eye, two, 0.0), axis=0, keepdims=True)
        part[k, 0:128, :] = jnp.where(upper, one, two)
        part[k, 128:256, :] = first[:, LANES : 2 * LANES]
        part[k, 256:384, :] = second[:, 3 * LANES :]
        part[k, 384:512, :] = first[:, 2 * LANES : 3 * LANES]
        part[k, 512:520, :] = jnp.broadcast_to(diagonal, (8, LANES))

    def side(odd):
        return 1 - 2 * odd

    def far(i, carry):
        gram(i)
        copy(part.at[i], r1.at[i], R1 + i, dev(fst + side(lax.rem(i, 2)), snd)).start()
        return carry

    lax.fori_loop(0, 4, far, 0)

    def near(i, carry):
        k = 4 + i
        gram(k)
        odd = lax.rem(i, 2)
        slot = odd * 4 + i + 1 - 2 * odd
        copy(part.at[k], r2.at[slot], R2 + slot, dev(fst + side(odd), snd)).start()
        return carry

    lax.fori_loop(0, 4, near, 0)

    def rest(i, carry):
        gram(8 + i)
        return carry

    lax.fori_loop(0, 8, rest, 0)

    def joined(i, carry):
        k = 8 + i
        odd = lax.rem(i, 2)
        slot = odd * 4 + i
        copy(part.at[i], r1.at[i], R1 + i, partner).wait_recv()
        part[k] = part[k] + r1[i]
        copy(part.at[k], r2.at[slot], R2 + slot, dev(fst + side(odd), snd)).start()
        return carry

    lax.fori_loop(0, 4, joined, 0)

    def arrived(b):
        for s in (0, 4):
            copy(r2.at[s + b], r2.at[s + b], R2 + s + b, partner).wait_recv()
        part[12 + b] = part[12 + b] + r2[b] + r2[4 + b]

    top = pl.ds(0, TOP)
    low = pl.ds(TOP, TRI - TOP)
    plus = dev(fst, snd + 1)
    minus = dev(fst, snd - 1)

    def second_copy(b, rows, into, place, device):
        return copy(part.at[12 + b, rows], into.at[rows], place, device)

    arrived(0)
    far_top = second_copy(0, top, r3, R3, plus)
    far_low = second_copy(0, low, r3, R3 + 1, minus)
    far_top.start()
    far_low.start()
    arrived(1)
    near_low = second_copy(1, low, r4.at[0], R4 + 1, plus)
    near_low.start()
    arrived(2)
    near_top = second_copy(2, top, r4.at[1], R4 + 2, minus)
    near_top.start()
    far_top.wait_recv()
    part[13, top] = part[13, top] + r3[top]
    join_top = second_copy(1, top, r4.at[0], R4, plus)
    join_top.start()
    far_low.wait_recv()
    part[14, low] = part[14, low] + r3[low]
    join_low = second_copy(2, low, r4.at[1], R4 + 3, minus)
    join_low.start()
    arrived(3)
    near_low.wait_recv()
    near_top.wait_recv()
    join_top.wait_recv()
    join_low.wait_recv()
    half[core] = (part[15] + r4[0] + r4[1]) * (1.0 / total_rows)
    exchange = copy(half.at[core], half.at[core], EXC, partner)
    exchange.start()

    def wait_query(i, carry):
        copy(qstage.at[i], qrx.at[i], QRY + i, partner).wait_recv()
        return carry

    lax.fori_loop(1, CHIPS, wait_query, 0)
    sub = lax.broadcasted_iota(jnp.int32, (8, WIDTH), 0)
    query = jnp.concatenate(
        [jnp.where(sub < 4, qrx[2 * t], qrx[2 * t + 1]) for t in range(CHIPS // 2)], axis=0
    )
    copy(half.at[1 - core], half.at[1 - core], EXC, partner).wait_recv()

    def block_at(a, b):
        return pl.ds(a * LANES, LANES), pl.ds(b * LANES, LANES)

    squares = jnp.zeros((LANES, LANES), F32)
    traces = jnp.zeros((LANES, LANES), F32)
    diagonals = {}
    for h in range(2):
        b0, b1, b2, b3 = [(i + h) % 4 for i in range(4)]
        packed = half[h, 0:128, :]
        packed_t = packed.T
        spare = jnp.broadcast_to(half[h, 512:513, :], (LANES, LANES))
        diagonals[b0] = jnp.where(upper, packed, packed_t)
        diagonals[b2] = jnp.where(eye, spare, jnp.where(upper, packed_t, packed))
        for start, a, b in ((128, b0, b1), (256, b2, b3), (384, b0, b2)):
            block = half[h, start : start + LANES, :]
            squares = squares + 2.0 * (block * block)
            p_ref[block_at(a, b)] = block
            p_ref[block_at(b, a)] = block.T
    for block in diagonals.values():
        traces = traces + jnp.where(eye, block, 0.0)
    shift = damp_ref[chip] * jnp.sum(traces) / WIDTH
    for a, block in diagonals.items():
        block = block + jnp.where(eye, shift, 0.0)
        squares = squares + block * block
        p_ref[block_at(a, a)] = block
    scaled = jnp.full((8, LANES), jnp.sum(squares) + EPSILON, F32)
    unit = (1.0 / jnp.sqrt(scaled))[0:1, 0:1]
    p_ref[...] = p_ref[...] * unit
    cond[core, chip] = query * unit

    def newton(step, carry):
        value = p_ref[...]
        vector = cond[core, chip]
        high, low_ = split(value)
        v_high, v_low = split(vector)
        left_hi = jnp.concatenate([high, v_high], axis=0)
        left_lo = jnp.concatenate([low_, v_low], axis=0)
        prod = dot(left_hi, high) + (dot(left_hi, low_) + dot(left_lo, high))
        p_ref[...] = 2.0 * value - prod[:WIDTH]
        cond[core, chip] = 2.0 * vector - prod[WIDTH:]
        return carry

    lax.fori_loop(0, NEWTON_STEPS - 2, newton, 0)
    high, low_ = split(p_ref[...])

    def apply(vector):
        v_high, v_low = split(vector)
        return dot(v_high, high) + (dot(v_high, low_) + dot(v_low, high))

    vector = cond[core, chip]
    vector = 2.0 * vector - apply(vector)
    once = apply(vector)
    vector = 2.0 * vector - (2.0 * once - apply(once))
    cond[core, chip] = vector

    upper_q = pl.ds(0, HALF_Q // 2)
    lower_q = pl.ds(HALF_Q // 2, HALF_Q // 2)

    def whole(p, q):
        return cond.at[core, chip_at(wrap(p), wrap(q))]

    def rows_of(p, q, rows):
        return cond.at[core, chip_at(wrap(p), wrap(q)), rows]

    sent = []

    def go(ref, place, device):
        c = copy(ref, ref, place, device)
        c.start()
        sent.append(c)

    def come(ref, place):
        copy(ref, ref, place, partner).wait_recv()

    first_plus = dev(fst + 1, snd)
    first_minus = dev(fst - 1, snd)

    def score(c, j):
        v_high, v_low = split(cond[c, j])
        got = dot_t(v_high, g_hi[j]) + (dot_t(v_high, g_lo[j]) + dot_t(v_low, g_hi[j]))
        rows = pl.ds(pl.multiple_of(c * HALF_Q, HALF_Q), HALF_Q)
        acc[rows, :] = acc[rows, :] + got

    def place_par(a, b):
        return PAR + a * 4 + b

    def hand_over(a, b):
        go(whole(fst + a, snd + b), place_par(a, b), partner)

    acc[...] = jnp.zeros((2 * HALF_Q, ROWS), F32)

    def along_first(b):
        go(whole(fst, snd + b), FST + 4 * b, first_plus)
        go(whole(fst, snd + b), FST + 4 * b + 1, first_minus)

    go(whole(fst, snd), SEC, plus)
    go(whole(fst, snd), SEC + 1, minus)
    along_first(0)
    hand_over(0, 0)
    come(whole(fst, snd - 1), SEC)
    go(rows_of(fst, snd - 1, upper_q), SEC + 2, plus)
    along_first(3)
    hand_over(0, 3)
    come(whole(fst, snd + 1), SEC + 1)
    go(rows_of(fst, snd + 1, lower_q), SEC + 3, minus)
    along_first(1)
    hand_over(0, 1)

    def first_near(b):
        come(whole(fst - 1, snd + b), FST + 4 * b)
        go(rows_of(fst - 1, snd + b, upper_q), FST + 4 * b + 2, first_plus)
        hand_over(3, b)
        come(whole(fst + 1, snd + b), FST + 4 * b + 1)
        go(rows_of(fst + 1, snd + b, lower_q), FST + 4 * b + 3, first_minus)
        hand_over(1, b)

    def first_far(b):
        come(rows_of(fst + 2, snd + b, upper_q), FST + 4 * b + 2)
        come(rows_of(fst + 2, snd + b, lower_q), FST + 4 * b + 3)
        hand_over(2, b)

    def own_scores(a, b):
        score(core, chip_at(wrap(fst + a), wrap(snd + b)))

    first_near(0)
    come(rows_of(fst, snd + 2, upper_q), SEC + 2)
    come(rows_of(fst, snd + 2, lower_q), SEC + 3)
    along_first(2)
    hand_over(0, 2)
    for b in (0, 3, 1, 2):
        own_scores(0, b)
    own_scores(1, 0)
    own_scores(3, 0)
    for before, b in ((0, 3), (3, 1), (1, 2)):
        first_near(b)
        first_far(before)
        own_scores(1, b)
        own_scores(3, b)
        own_scores(2, before)
    first_far(2)
    own_scores(2, 2)

    def other(a, b):
        c = 1 - core
        j = chip_at(wrap(snd + a), wrap(fst + b), c)
        come(cond.at[c, j], place_par(a, b))
        score(c, j)

    for b in (0, 3, 1):
        other(0, b)
    other(3, 0)
    other(1, 0)
    other(0, 2)
    for before, b in ((0, 3), (3, 1), (1, 2)):
        other(3, b)
        other(1, b)
        other(2, before)
    other(2, 2)

    done = acc[...] * scale
    for h in range(2):
        zout[:, 8 * h : 8 * h + 8, :] = done[h * HALF_Q : (h + 1) * HALF_Q].reshape(DEPTH, 8, ROWS)

    def send_scores(i, carry):
        there = lax.rem(z + i, DEPTH)
        copy(zout.at[there], zin.at[i], ZED + i, (there, dp)).start()
        return carry

    lax.fori_loop(1, DEPTH, send_scores, 0)
    total = zout[z]
    for i in range(1, DEPTH):
        copy(zin.at[i], zin.at[i], ZED + i, partner).wait_recv()
        total = total + zin[i]
    out_ref[...] = jnp.concatenate([total[0:4], total[8:12], total[4:8], total[12:16]], axis=0)

    def sent_raw(k, carry):
        copy(stage.at[0], rx.at[0], RAW + k, partner).wait_send()
        return carry

    lax.fori_loop(0, CHIPS, sent_raw, 0)

    def sent_query(i, carry):
        copy(qstage.at[0], qrx.at[0], QRY + i, partner).wait_send()
        return carry

    lax.fori_loop(1, CHIPS, sent_query, 0)

    def sent_part(i, carry):
        copy(part.at[0], r2.at[0], R1 + i, partner).wait_send()
        return carry

    lax.fori_loop(0, 12, sent_part, 0)
    for c in (far_top, far_low, near_low, near_top, join_top, join_low, exchange, *sent):
        c.wait_send()

    def sent_scores(i, carry):
        copy(zout.at[0], zin.at[0], ZED + i, partner).wait_send()
        return carry

    lax.fori_loop(1, DEPTH, sent_scores, 0)


def per_device(train_grads, queries, damping):
    rows, modules, width = train_grads.shape
    total_rows = rows * lax.axis_size("dp")
    scale = 1.0 / math.sqrt(modules * lax.axis_size("mod") * width)
    vmem = pltpu.VMEM
    out = pl.pallas_call(
        functools.partial(kernel, total_rows, scale),
        out_shape=jax.ShapeDtypeStruct((16, ROWS), F32),
        in_specs=[
            pl.BlockSpec(memory_space=pl.ANY),
            pl.BlockSpec(memory_space=pl.ANY),
            pl.BlockSpec(memory_space=pltpu.SMEM),
        ],
        out_specs=pl.BlockSpec(memory_space=vmem),
        scratch_shapes=[
            vmem((4, ROWS * CHIPS, LANES), F32),
            vmem((4, 4 * CHIPS, LANES), F32),
            vmem((CHIPS, ROWS, WIDTH), F32),
            vmem((CHIPS, ROWS, WIDTH), F32),
            vmem((CHIPS, 8, WIDTH), F32),
            vmem((CHIPS, 8, WIDTH), F32),
            vmem((CHIPS, TRI, LANES), F32),
            vmem((4, TRI, LANES), F32),
            vmem((8, TRI, LANES), F32),
            vmem((TRI, LANES), F32),
            vmem((2, TRI, LANES), F32),
            vmem((2, TRI, LANES), F32),
            vmem((WIDTH, WIDTH), F32),
            vmem((2, CHIPS, HALF_Q, WIDTH), F32),
            vmem((CHIPS, ROWS, WIDTH), BF16),
            vmem((CHIPS, ROWS, WIDTH), BF16),
            vmem((2 * HALF_Q, ROWS), F32),
            vmem((DEPTH, 16, ROWS), F32),
            vmem((DEPTH, 16, ROWS), F32),
            pltpu.SemaphoreType.DMA((8,)),
            pltpu.SemaphoreType.DMA((COPIES,)),
            pltpu.SemaphoreType.DMA((COPIES,)),
        ],
        compiler_params=pltpu.CompilerParams(
            collective_id=0, has_side_effects=True, vmem_limit_bytes=60 * 2**20
        ),
    )(train_grads.reshape(rows * modules, width), queries.reshape(-1, width), damping)
    return out.T


def solution(mesh):
    return jax.shard_map(
        per_device,
        mesh=mesh,
        in_specs=(P("dp", "mod", None), P("dp", "mod", None), P("mod")),
        out_specs=P("dp", "mod"),
        check_vma=False,
    )
```

```python
import functools
import math

import jax
import jax.numpy as jnp
from jax import lax
from jax.experimental import pallas as pl
from jax.experimental.pallas import tpu as pltpu
from jax.sharding import PartitionSpec as P

NEWTON_STEPS = 8
EPSILON = 1e-06

SIDE = 4
CHIPS = SIDE * SIDE
DEPTH = 8
WIDTH = 512
ROWS = 128
LANES = 128
MID = WIDTH // 2
TRI = 4 * LANES + 8
TOP = 264
HALF_Q = 64
BF16 = jnp.bfloat16
F32 = jnp.float32

RAW = 0
QRY = RAW + 16
R1 = QRY + 16
R2 = R1 + 4
R3 = R2 + 8
R4 = R3 + 2
EXC = R4 + 4
SEC = EXC + 1
FST = SEC + 6
PAR = FST + 24
ZED = PAR + 16
COPIES = ZED + 8


def split(value):
    high = value.astype(BF16)
    return high, (value - high.astype(F32)).astype(BF16)


def dot(a, b):
    return jnp.dot(a, b, preferred_element_type=F32)


def dot_t(a, b):
    return lax.dot_general(a, b, (((1,), (1,)), ((), ())), preferred_element_type=F32)


def wrap(i):
    return lax.rem(i + 2 * SIDE, SIDE)


def kernel(
    total_rows,
    scale,
    x_hbm,
    q_hbm,
    damp_ref,
    out_ref,
    x,
    q_in,
    stage,
    rx,
    qstage,
    qrx,
    part,
    r1,
    r2,
    r3,
    r4,
    half,
    p_ref,
    cond,
    grads,
    acc,
    zout,
    zin,
    in_sem,
    send,
    recv,
):
    z = lax.axis_index("mod")
    dp = lax.axis_index("dp")
    core = lax.rem(dp, 2)
    chip = lax.div(dp, 2)
    cx = lax.div(chip, SIDE)
    cy = lax.rem(chip, SIDE)
    fst = cx * (1 - core) + cy * core
    snd = cy * (1 - core) + cx * core

    def chip_at(p, q, c=core):
        return (p * (1 - c) + q * c) * SIDE + q * (1 - c) + p * c

    def dev(p, q):
        return (z, chip_at(wrap(p), wrap(q)) * 2 + core)

    partner = (z, chip * 2 + 1 - core)

    def copy(src, dst, place, device):
        return pltpu.make_async_remote_copy(
            src_ref=src,
            dst_ref=dst,
            send_sem=send.at[place],
            recv_sem=recv.at[place],
            device_id=device,
            device_id_type=pl.DeviceIdType.MESH,
        )

    loads = []
    for lb in range(4):
        cols = pl.ds(lb * LANES, LANES)
        loads.append(pltpu.make_async_copy(x_hbm.at[:, cols], x.at[lb], in_sem.at[lb]))
        loads.append(pltpu.make_async_copy(q_hbm.at[:, cols], q_in.at[lb], in_sem.at[4 + lb]))
    for load in loads:
        load.start()

    barrier = pltpu.get_barrier_semaphore()

    def greet_chip(i, carry):
        there = lax.rem(chip + i, CHIPS)
        pl.semaphore_signal(
            barrier, inc=1, device_id=(z, there * 2 + core), device_id_type=pl.DeviceIdType.MESH
        )
        return carry

    lax.fori_loop(1, CHIPS, greet_chip, 0)

    def greet_layer(i, carry):
        pl.semaphore_signal(
            barrier, inc=1, device_id=(lax.rem(z + i, DEPTH), dp), device_id_type=pl.DeviceIdType.MESH
        )
        return carry

    lax.fori_loop(1, DEPTH, greet_layer, 0)
    pl.semaphore_signal(barrier, inc=1, device_id=partner, device_id_type=pl.DeviceIdType.MESH)
    def second_of(b):
        return lax.rem(2 + 3 * b + lax.div(b, 2) * (3 - 2 * lax.rem(b, 2)), SIDE)

    def order(k):
        is0 = lax.div(CHIPS - 1 - k, 12)
        is3 = lax.div(k, 12)
        i = (k - 4) * (1 - is0) * (1 - is3)
        first = is0 * 2 + (1 - is0 - is3) * (1 + 2 * lax.rem(i, 2))
        late = lax.div(i, 4)
        middle = late * lax.div(i, 2) + (1 - late) * (1 - lax.rem(lax.div(i + 1, 2), 2))
        b = (is0 + is3) * lax.rem(k, 4) + (1 - is0 - is3) * middle
        return first, b

    def module_of(k, c):
        first, b = order(k)
        p = cx * (1 - c) + cy * c
        q = cy * (1 - c) + cx * c
        return chip_at(lax.rem(p + first, SIDE), lax.rem(q + second_of(b), SIDE), c)

    for load in loads:
        load.wait()

    def stage_module(j, carry):
        for lb in range(4):
            stage[j, :, pl.ds(lb * LANES, LANES)] = x[lb, pl.ds(j, ROWS, stride=CHIPS), :]
            qstage[j, pl.ds(lb * 4, 4), :] = q_in[lb, pl.ds(j, 4, stride=CHIPS), :]
        return carry

    lax.fori_loop(0, CHIPS, stage_module, 0)
    pl.semaphore_wait(barrier, CHIPS - 1 + DEPTH - 1 + 1)

    def send_raw(k, carry):
        j = module_of(k, 1 - core)
        copy(stage.at[j], rx.at[j], RAW + k, partner).start()
        return carry

    lax.fori_loop(0, 4, send_raw, 0)

    def send_query(i, carry):
        there = lax.rem(chip + i, CHIPS)
        copy(qstage.at[there], qrx.at[chip], QRY + i, (z, there * 2 + core)).start()
        return carry

    lax.fori_loop(1, CHIPS, send_query, 0)
    lax.fori_loop(4, CHIPS, send_raw, 0)
    qrx[chip] = qstage[chip]

    row_of = lax.broadcasted_iota(jnp.int32, (LANES, LANES), 0)
    col_of = lax.broadcasted_iota(jnp.int32, (LANES, LANES), 1)
    upper = row_of <= col_of
    eye = row_of == col_of

    def gram(k):
        j = module_of(k, core)
        copy(stage.at[j], rx.at[j], RAW + k, partner).wait_recv()
        blocks, highs, lows = [], [], []
        for lb in range(4):
            cols = pl.ds(pl.multiple_of(lax.rem(lb + core, 4) * LANES, LANES), LANES)
            block = jnp.concatenate([stage[j, :, cols], rx[j, :, cols]], axis=0)
            high, low = split(block)
            grads[j, :ROWS, cols] = high[:ROWS]
            grads[j, ROWS:, cols] = low[:ROWS]
            blocks.append(block)
            highs.append(high)
            lows.append(low)
        left = jnp.concatenate([blocks[0].T, blocks[2].T], axis=0)
        left_hi, left_lo = split(left)
        right_hi = jnp.concatenate(highs, axis=1)
        right_lo = jnp.concatenate(lows, axis=1)
        prod = dot(left_hi, right_hi) + (dot(left_hi, right_lo) + dot(left_lo, right_hi))
        first, second = prod[:LANES], prod[LANES:]
        one, two = first[:, :LANES], second[:, 2 * LANES : 3 * LANES]
        diagonal = jnp.sum(jnp.where(eye, two, 0.0), axis=0, keepdims=True)
        part[k, 0:128, :] = jnp.where(upper, one, two)
        part[k, 128:256, :] = first[:, LANES : 2 * LANES]
        part[k, 256:384, :] = second[:, 3 * LANES :]
        part[k, 384:512, :] = first[:, 2 * LANES : 3 * LANES]
        part[k, 512:520, :] = jnp.broadcast_to(diagonal, (8, LANES))

    def side(odd):
        return 1 - 2 * odd

    def far(i, carry):
        gram(i)
        copy(part.at[i], r1.at[i], R1 + i, dev(fst + side(lax.rem(i, 2)), snd)).start()
        return carry

    lax.fori_loop(0, 4, far, 0)

    def grams(low, high):
        def step(k, carry):
            gram(k)
            return carry

        lax.fori_loop(low, high, step, 0)

    def near(k, slot):
        copy(part.at[k], r2.at[slot], R2 + slot, dev(fst + (1 if slot < 4 else -1), snd)).start()

    def joined(k, i, slot):
        copy(part.at[i], r1.at[i], R1 + i, partner).wait_recv()
        part[k] = part[k] + r1[i]
        near(k, slot)

    grams(4, 5)
    near(4, 1)
    grams(5, 6)
    near(5, 4)
    grams(6, 12)
    joined(6, 0, 0)
    joined(7, 1, 5)
    near(9, 6)
    grams(12, 16)
    joined(8, 2, 2)
    near(10, 3)
    joined(11, 3, 7)

    def arrived(b):
        for s in (0, 4):
            copy(r2.at[s + b], r2.at[s + b], R2 + s + b, partner).wait_recv()
        part[12 + b] = part[12 + b] + r2[b] + r2[4 + b]

    def wait_query(i, carry):
        copy(qstage.at[i], qrx.at[i], QRY + i, partner).wait_recv()
        return carry

    lax.fori_loop(1, CHIPS, wait_query, 0)
    for lb in range(4):
        cond[core, chip, :, lb * LANES : (lb + 1) * LANES] = jnp.concatenate(
            [qrx[i, lb * 4 : lb * 4 + 4, :] for i in range(CHIPS)], axis=0
        )

    top = pl.ds(0, TOP)
    low = pl.ds(TOP, TRI - TOP)
    plus = dev(fst, snd + 1)
    minus = dev(fst, snd - 1)

    def second_copy(b, rows, into, place, device):
        return copy(part.at[12 + b, rows], into.at[rows], place, device)

    arrived(0)
    far_top = second_copy(0, top, r3, R3, plus)
    far_low = second_copy(0, low, r3, R3 + 1, minus)
    far_top.start()
    far_low.start()
    arrived(1)
    near_low = second_copy(1, low, r4.at[0], R4 + 1, plus)
    near_low.start()
    arrived(2)
    near_top = second_copy(2, top, r4.at[1], R4 + 2, minus)
    near_top.start()
    far_top.wait_recv()
    part[13, top] = part[13, top] + r3[top]
    join_top = second_copy(1, top, r4.at[0], R4, plus)
    join_top.start()
    far_low.wait_recv()
    part[14, low] = part[14, low] + r3[low]
    join_low = second_copy(2, low, r4.at[1], R4 + 3, minus)
    join_low.start()
    arrived(3)
    near_low.wait_recv()
    near_top.wait_recv()
    join_top.wait_recv()
    join_low.wait_recv()
    half[core] = (part[15] + r4[0] + r4[1]) * (1.0 / total_rows)
    exchange = copy(half.at[core], half.at[core], EXC, partner)
    exchange.start()

    copy(half.at[1 - core], half.at[1 - core], EXC, partner).wait_recv()

    def block_at(a, b):
        return pl.ds(a * LANES, LANES), pl.ds(b * LANES, LANES)

    squares = jnp.zeros((LANES, LANES), F32)
    traces = jnp.zeros((LANES, LANES), F32)
    diagonals = {}
    for h in range(2):
        b0, b1, b2, b3 = [(i + h) % 4 for i in range(4)]
        packed = half[h, 0:128, :]
        packed_t = packed.T
        spare = jnp.broadcast_to(half[h, 512:513, :], (LANES, LANES))
        diagonals[b0] = jnp.where(upper, packed, packed_t)
        diagonals[b2] = jnp.where(eye, spare, jnp.where(upper, packed_t, packed))
        for start, a, b in ((128, b0, b1), (256, b2, b3), (384, b0, b2)):
            block = half[h, start : start + LANES, :]
            squares = squares + 2.0 * (block * block)
            p_ref[block_at(a, b)] = block
            p_ref[block_at(b, a)] = block.T
    for block in diagonals.values():
        traces = traces + jnp.where(eye, block, 0.0)
    shift = damp_ref[chip] * jnp.sum(traces) / WIDTH
    for a, block in diagonals.items():
        block = block + jnp.where(eye, shift, 0.0)
        squares = squares + block * block
        p_ref[block_at(a, a)] = block
    scaled = jnp.full((8, LANES), jnp.sum(squares) + EPSILON, F32)
    unit = (1.0 / jnp.sqrt(scaled))[0:1, 0:1]
    p_ref[...] = p_ref[...] * unit
    cond[core, chip] = cond[core, chip] * unit

    def newton(step, carry):
        value = p_ref[...]
        vector = cond[core, chip]
        high, low_ = split(value)
        v_high, v_low = split(vector)
        left_hi = jnp.concatenate([high[:MID], v_high], axis=0)
        left_lo = jnp.concatenate([low_[:MID], v_low], axis=0)
        prod = dot(left_hi, high) + (dot(left_hi, low_) + dot(left_lo, high))
        hi_r, lo_r = high[:, MID:], low_[:, MID:]
        corner = dot(high[MID:], hi_r) + (dot(high[MID:], lo_r) + dot(low_[MID:], hi_r))
        upper_rows = 2.0 * value[:MID] - prod[:MID]
        p_ref[:MID, :] = upper_rows
        p_ref[MID:, :MID] = upper_rows[:, MID:].T
        p_ref[MID:, MID:] = 2.0 * value[MID:, MID:] - corner
        cond[core, chip] = 2.0 * vector - prod[MID:]
        return carry

    lax.fori_loop(0, NEWTON_STEPS - 2, newton, 0)
    high, low_ = split(p_ref[...])

    def apply(vector):
        v_high, v_low = split(vector)
        return dot(v_high, high) + (dot(v_high, low_) + dot(v_low, high))

    vector = cond[core, chip]
    vector = 2.0 * vector - apply(vector)
    once = apply(vector)
    vector = 2.0 * vector - (2.0 * once - apply(once))
    cond[core, chip] = vector

    halves = (pl.ds(0, HALF_Q // 2), pl.ds(HALF_Q // 2, HALF_Q // 2))
    first_to = (dev(fst + 1, snd), dev(fst - 1, snd))
    second_to = (plus, minus)
    sent = []

    def at(a, b, rows=None):
        ref = cond.at[core, chip_at(wrap(fst + a), wrap(snd + b))]
        return ref if rows is None else ref.at[rows]

    def go(ref, place, device):
        c = copy(ref, ref, place, device)
        c.start()
        sent.append(c)

    def come(ref, place):
        copy(ref, ref, place, partner).wait_recv()

    def hand_over(a, b):
        go(at(a, b), PAR + a * 4 + b, partner)

    def both_ways(a, b, place, devices):
        for n in range(2):
            for way in range(2):
                h = n ^ way
                go(at(a, b, halves[h]), place + 2 * way + n, devices[way])

    def along_first(b):
        both_ways(0, b, FST + 6 * b, first_to)

    def pass_first(b):
        for way in range(2):
            come(at(3 - 2 * way, b, halves[way]), FST + 6 * b + 2 * way)
            go(at(3 - 2 * way, b, halves[way]), FST + 6 * b + 4 + way, first_to[way])

    def rest_first(b):
        for way in range(2):
            come(at(3 - 2 * way, b, halves[1 - way]), FST + 6 * b + 2 * way + 1)
            hand_over(3 - 2 * way, b)

    def far_first(b):
        for way in range(2):
            come(at(2, b, halves[way]), FST + 6 * b + 4 + way)
        hand_over(2, b)

    def score(c, j):
        left = jnp.concatenate(split(cond[c, j]), axis=0)
        got = dot_t(left, grads[j])
        got = got[:, :ROWS] + got[:, ROWS:]
        rows = pl.ds(pl.multiple_of(c * HALF_Q, HALF_Q), HALF_Q)
        acc[rows, :] = acc[rows, :] + (got[:HALF_Q] + got[HALF_Q:])

    def own(a, b):
        score(core, chip_at(wrap(fst + a), wrap(snd + b)))

    def other(a, b):
        c = 1 - core
        j = chip_at(wrap(snd + a), wrap(fst + b), c)
        come(cond.at[c, j], PAR + a * 4 + b)
        score(c, j)

    acc[...] = jnp.zeros((2 * HALF_Q, ROWS), F32)
    both_ways(0, 0, SEC, second_to)
    along_first(0)
    hand_over(0, 0)
    for way in range(2):
        come(at(0, 3 - 2 * way, halves[way]), SEC + 2 * way)
        go(at(0, 3 - 2 * way, halves[way]), SEC + 4 + way, second_to[way])
    for way in range(2):
        come(at(0, 3 - 2 * way, halves[1 - way]), SEC + 2 * way + 1)
        along_first(3 - 2 * way)
        hand_over(0, 3 - 2 * way)
    pass_first(0)
    rest_first(0)
    own(0, 0)
    for way in range(2):
        come(at(0, 2, halves[way]), SEC + 4 + way)
    along_first(2)
    hand_over(0, 2)
    own(0, 3)
    own(0, 1)
    other(0, 0)
    pass_first(3)
    rest_first(3)
    own(0, 2)
    own(3, 0)
    pass_first(1)
    rest_first(1)
    own(1, 0)
    other(0, 3)
    far_first(0)
    other(0, 1)
    pass_first(2)
    rest_first(2)
    own(3, 3)
    own(1, 3)
    other(3, 0)
    other(1, 0)
    far_first(3)
    own(3, 1)
    own(1, 1)
    other(0, 2)
    far_first(1)
    own(2, 0)
    other(3, 3)
    other(1, 3)
    far_first(2)
    for a, b in ((3, 2), (1, 2), (2, 3), (2, 1)):
        own(a, b)
    for a, b in ((3, 1), (1, 1), (2, 0), (3, 2), (1, 2)):
        other(a, b)
    own(2, 2)
    for b in (3, 1, 2):
        other(2, b)

    done = acc[...] * scale
    for h in range(2):
        zout[:, 8 * h : 8 * h + 8, :] = done[h * HALF_Q : (h + 1) * HALF_Q].reshape(DEPTH, 8, ROWS)

    def send_scores(i, carry):
        there = lax.rem(z + i, DEPTH)
        copy(zout.at[there], zin.at[i], ZED + i, (there, dp)).start()
        return carry

    lax.fori_loop(1, DEPTH, send_scores, 0)
    total = zout[z]
    for i in range(1, DEPTH):
        copy(zin.at[i], zin.at[i], ZED + i, partner).wait_recv()
        total = total + zin[i]
    out_ref[...] = jnp.concatenate([total[0:4], total[8:12], total[4:8], total[12:16]], axis=0)

    def sent_raw(k, carry):
        copy(stage.at[0], rx.at[0], RAW + k, partner).wait_send()
        return carry

    lax.fori_loop(0, CHIPS, sent_raw, 0)

    def sent_query(i, carry):
        copy(qstage.at[0], qrx.at[0], QRY + i, partner).wait_send()
        return carry

    lax.fori_loop(1, CHIPS, sent_query, 0)

    def sent_part(i, carry):
        copy(part.at[0], r2.at[0], R1 + i, partner).wait_send()
        return carry

    lax.fori_loop(0, 12, sent_part, 0)
    for c in (far_top, far_low, near_low, near_top, join_top, join_low, exchange, *sent):
        c.wait_send()

    def sent_scores(i, carry):
        copy(zout.at[0], zin.at[0], ZED + i, partner).wait_send()
        return carry

    lax.fori_loop(1, DEPTH, sent_scores, 0)


def per_device(train_grads, queries, damping):
    rows, modules, width = train_grads.shape
    total_rows = rows * lax.axis_size("dp")
    scale = 1.0 / math.sqrt(modules * lax.axis_size("mod") * width)
    vmem = pltpu.VMEM
    out = pl.pallas_call(
        functools.partial(kernel, total_rows, scale),
        out_shape=jax.ShapeDtypeStruct((16, ROWS), F32),
        in_specs=[
            pl.BlockSpec(memory_space=pl.ANY),
            pl.BlockSpec(memory_space=pl.ANY),
            pl.BlockSpec(memory_space=pltpu.SMEM),
        ],
        out_specs=pl.BlockSpec(memory_space=vmem),
        scratch_shapes=[
            vmem((4, ROWS * CHIPS, LANES), F32),
            vmem((4, 4 * CHIPS, LANES), F32),
            vmem((CHIPS, ROWS, WIDTH), F32),
            vmem((CHIPS, ROWS, WIDTH), F32),
            vmem((CHIPS, 16, LANES), F32),
            vmem((CHIPS, 16, LANES), F32),
            vmem((CHIPS, TRI, LANES), F32),
            vmem((4, TRI, LANES), F32),
            vmem((8, TRI, LANES), F32),
            vmem((TRI, LANES), F32),
            vmem((2, TRI, LANES), F32),
            vmem((2, TRI, LANES), F32),
            vmem((WIDTH, WIDTH), F32),
            vmem((2, CHIPS, HALF_Q, WIDTH), F32),
            vmem((CHIPS, 2 * ROWS, WIDTH), BF16),
            vmem((2 * HALF_Q, ROWS), F32),
            vmem((DEPTH, 16, ROWS), F32),
            vmem((DEPTH, 16, ROWS), F32),
            pltpu.SemaphoreType.DMA((8,)),
            pltpu.SemaphoreType.DMA((COPIES,)),
            pltpu.SemaphoreType.DMA((COPIES,)),
        ],
        compiler_params=pltpu.CompilerParams(
            collective_id=0, has_side_effects=True, vmem_limit_bytes=60 * 2**20
        ),
    )(train_grads.reshape(rows * modules, width), queries.reshape(-1, width), damping)
    return out.T


def solution(mesh):
    return jax.shard_map(
        per_device,
        mesh=mesh,
        in_specs=(P("dp", "mod", None), P("dp", "mod", None), P("mod")),
        out_specs=P("dp", "mod"),
        check_vma=False,
    )
```

```python
import functools
import math

import jax
import jax.numpy as jnp
from jax import lax
from jax.experimental import pallas as pl
from jax.experimental.pallas import tpu as pltpu
from jax.sharding import PartitionSpec as P

NEWTON_STEPS = 8
EPSILON = 1e-06

SIDE = 4
CHIPS = SIDE * SIDE
DEPTH = 8
WIDTH = 512
ROWS = 128
LANES = 128
MID = WIDTH // 2
TRI = 4 * LANES + 8
TOP = 264
HALF_Q = 64
BF16 = jnp.bfloat16
F32 = jnp.float32

RAW = 0
QRY = RAW + 16
R1 = QRY + 16
R2 = R1 + 4
R3 = R2 + 8
R4 = R3 + 2
EXC = R4 + 4
SEC = EXC + 1
FST = SEC + 6
PAR = FST + 24
ZED = PAR + 16
COPIES = ZED + 8


def split(value):
    high = value.astype(BF16)
    return high, (value - high.astype(F32)).astype(BF16)


def dot(a, b):
    return jnp.dot(a, b, preferred_element_type=F32)


def dot_t(a, b):
    return lax.dot_general(a, b, (((1,), (1,)), ((), ())), preferred_element_type=F32)


def wrap(i):
    return lax.rem(i + 2 * SIDE, SIDE)


def kernel(
    total_rows,
    scale,
    x_hbm,
    q_hbm,
    damp_ref,
    out_ref,
    x,
    q_in,
    stage,
    rx,
    qstage,
    qrx,
    part,
    r1,
    r2,
    r3,
    r4,
    half,
    p_ref,
    cond,
    grads,
    acc,
    zout,
    zin,
    in_sem,
    send,
    recv,
):
    z = lax.axis_index("mod")
    dp = lax.axis_index("dp")
    core = lax.rem(dp, 2)
    chip = lax.div(dp, 2)
    cx = lax.div(chip, SIDE)
    cy = lax.rem(chip, SIDE)
    fst = cx * (1 - core) + cy * core
    snd = cy * (1 - core) + cx * core

    def chip_at(p, q, c=core):
        return (p * (1 - c) + q * c) * SIDE + q * (1 - c) + p * c

    def dev(p, q):
        return (z, chip_at(wrap(p), wrap(q)) * 2 + core)

    partner = (z, chip * 2 + 1 - core)

    def copy(src, dst, place, device):
        return pltpu.make_async_remote_copy(
            src_ref=src,
            dst_ref=dst,
            send_sem=send.at[place],
            recv_sem=recv.at[place],
            device_id=device,
            device_id_type=pl.DeviceIdType.MESH,
        )

    loads = []
    for lb in range(4):
        cols = pl.ds(lb * LANES, LANES)
        loads.append(pltpu.make_async_copy(x_hbm.at[:, cols], x.at[lb], in_sem.at[lb]))
        loads.append(pltpu.make_async_copy(q_hbm.at[:, cols], q_in.at[lb], in_sem.at[4 + lb]))
    for load in loads:
        load.start()

    barrier = pltpu.get_barrier_semaphore()

    def greet_chip(i, carry):
        there = lax.rem(chip + i, CHIPS)
        pl.semaphore_signal(
            barrier, inc=1, device_id=(z, there * 2 + core), device_id_type=pl.DeviceIdType.MESH
        )
        return carry

    lax.fori_loop(1, CHIPS, greet_chip, 0)

    def greet_layer(i, carry):
        pl.semaphore_signal(
            barrier, inc=1, device_id=(lax.rem(z + i, DEPTH), dp), device_id_type=pl.DeviceIdType.MESH
        )
        return carry

    lax.fori_loop(1, DEPTH, greet_layer, 0)
    pl.semaphore_signal(barrier, inc=1, device_id=partner, device_id_type=pl.DeviceIdType.MESH)
    def second_of(b):
        return lax.rem(2 + 3 * b + lax.div(b, 2) * (3 - 2 * lax.rem(b, 2)), SIDE)

    def order(k):
        is0 = lax.div(CHIPS - 1 - k, 12)
        is3 = lax.div(k, 12)
        i = (k - 4) * (1 - is0) * (1 - is3)
        first = is0 * 2 + (1 - is0 - is3) * (1 + 2 * lax.rem(i, 2))
        late = lax.div(i, 4)
        middle = late * lax.div(i, 2) + (1 - late) * (1 - lax.rem(lax.div(i + 1, 2), 2))
        b = (is0 + is3) * lax.rem(k, 4) + (1 - is0 - is3) * middle
        return first, b

    def module_of(k, c):
        first, b = order(k)
        p = cx * (1 - c) + cy * c
        q = cy * (1 - c) + cx * c
        return chip_at(lax.rem(p + first, SIDE), lax.rem(q + second_of(b), SIDE), c)

    for load in loads:
        load.wait()

    def stage_rows(k):
        j = module_of(k, 1 - core)
        for lb in range(4):
            stage[j, :, pl.ds(lb * LANES, LANES)] = x[lb, pl.ds(j, ROWS, stride=CHIPS), :]

    def stage_first(k, carry):
        stage_rows(k)
        return carry

    def stage_query(j, carry):
        for lb in range(4):
            qstage[j, pl.ds(lb * 4, 4), :] = q_in[lb, pl.ds(j, 4, stride=CHIPS), :]
        return carry

    lax.fori_loop(0, 4, stage_first, 0)
    lax.fori_loop(0, CHIPS, stage_query, 0)
    pl.semaphore_wait(barrier, CHIPS - 1 + DEPTH - 1 + 1)

    def send_raw(k, carry):
        j = module_of(k, 1 - core)
        copy(stage.at[j], rx.at[j], RAW + k, partner).start()
        return carry

    def stage_and_send(k, carry):
        stage_rows(k)
        return send_raw(k, carry)

    lax.fori_loop(0, 4, send_raw, 0)

    def send_query(i, carry):
        there = lax.rem(chip + i, CHIPS)
        copy(qstage.at[there], qrx.at[chip], QRY + i, (z, there * 2 + core)).start()
        return carry

    lax.fori_loop(1, CHIPS, send_query, 0)
    lax.fori_loop(4, CHIPS, stage_and_send, 0)
    qrx[chip] = qstage[chip]

    row_of = lax.broadcasted_iota(jnp.int32, (LANES, LANES), 0)
    col_of = lax.broadcasted_iota(jnp.int32, (LANES, LANES), 1)
    upper = row_of <= col_of
    eye = row_of == col_of

    def gram(k):
        j = module_of(k, core)
        copy(stage.at[j], rx.at[j], RAW + k, partner).wait_recv()
        blocks, highs, lows = [], [], []
        for lb in range(4):
            cols = pl.ds(pl.multiple_of(lax.rem(lb + core, 4) * LANES, LANES), LANES)
            block = jnp.concatenate([stage[j, :, cols], rx[j, :, cols]], axis=0)
            high, low = split(block)
            grads[j, :ROWS, cols] = high[:ROWS]
            grads[j, ROWS:, cols] = low[:ROWS]
            blocks.append(block)
            highs.append(high)
            lows.append(low)
        left = jnp.concatenate([blocks[0].T, blocks[2].T], axis=0)
        left_hi, left_lo = split(left)
        right_hi = jnp.concatenate(highs, axis=1)
        right_lo = jnp.concatenate(lows, axis=1)
        prod = dot(left_hi, right_hi) + (dot(left_hi, right_lo) + dot(left_lo, right_hi))
        first, second = prod[:LANES], prod[LANES:]
        one, two = first[:, :LANES], second[:, 2 * LANES : 3 * LANES]
        diagonal = jnp.sum(jnp.where(eye, two, 0.0), axis=0, keepdims=True)
        part[k, 0:128, :] = jnp.where(upper, one, two)
        part[k, 128:256, :] = first[:, LANES : 2 * LANES]
        part[k, 256:384, :] = second[:, 3 * LANES :]
        part[k, 384:512, :] = first[:, 2 * LANES : 3 * LANES]
        part[k, 512:520, :] = jnp.broadcast_to(diagonal, (8, LANES))

    def side(odd):
        return 1 - 2 * odd

    def far(i, carry):
        gram(i)
        copy(part.at[i], r1.at[i], R1 + i, dev(fst + side(lax.rem(i, 2)), snd)).start()
        return carry

    lax.fori_loop(0, 4, far, 0)

    def grams(low, high):
        def step(k, carry):
            gram(k)
            return carry

        lax.fori_loop(low, high, step, 0)

    def near(k, slot):
        copy(part.at[k], r2.at[slot], R2 + slot, dev(fst + (1 if slot < 4 else -1), snd)).start()

    def joined(k, i, slot):
        copy(part.at[i], r1.at[i], R1 + i, partner).wait_recv()
        part[k] = part[k] + r1[i]
        near(k, slot)

    grams(4, 5)
    near(4, 1)
    grams(5, 6)
    near(5, 4)
    grams(6, 12)
    joined(6, 0, 0)
    joined(7, 1, 5)
    near(9, 6)
    grams(12, 16)
    joined(8, 2, 2)
    near(10, 3)
    joined(11, 3, 7)

    def arrived(b):
        for s in (0, 4):
            copy(r2.at[s + b], r2.at[s + b], R2 + s + b, partner).wait_recv()
        part[12 + b] = part[12 + b] + r2[b] + r2[4 + b]

    def wait_query(i, carry):
        copy(qstage.at[i], qrx.at[i], QRY + i, partner).wait_recv()
        return carry

    lax.fori_loop(1, CHIPS, wait_query, 0)
    for lb in range(4):
        cond[core, chip, :, lb * LANES : (lb + 1) * LANES] = jnp.concatenate(
            [qrx[i, lb * 4 : lb * 4 + 4, :] for i in range(CHIPS)], axis=0
        )

    top = pl.ds(0, TOP)
    low = pl.ds(TOP, TRI - TOP)
    plus = dev(fst, snd + 1)
    minus = dev(fst, snd - 1)

    def second_copy(b, rows, into, place, device):
        return copy(part.at[12 + b, rows], into.at[rows], place, device)

    arrived(0)
    far_top = second_copy(0, top, r3, R3, plus)
    far_low = second_copy(0, low, r3, R3 + 1, minus)
    far_top.start()
    far_low.start()
    arrived(1)
    near_low = second_copy(1, low, r4.at[0], R4 + 1, plus)
    near_low.start()
    arrived(2)
    near_top = second_copy(2, top, r4.at[1], R4 + 2, minus)
    near_top.start()
    far_top.wait_recv()
    part[13, top] = part[13, top] + r3[top]
    join_top = second_copy(1, top, r4.at[0], R4, plus)
    join_top.start()
    far_low.wait_recv()
    part[14, low] = part[14, low] + r3[low]
    join_low = second_copy(2, low, r4.at[1], R4 + 3, minus)
    join_low.start()
    arrived(3)
    near_low.wait_recv()
    near_top.wait_recv()
    join_top.wait_recv()
    join_low.wait_recv()
    half[core] = (part[15] + r4[0] + r4[1]) * (1.0 / total_rows)
    exchange = copy(half.at[core], half.at[core], EXC, partner)
    exchange.start()

    copy(half.at[1 - core], half.at[1 - core], EXC, partner).wait_recv()

    def block_at(a, b):
        return pl.ds(a * LANES, LANES), pl.ds(b * LANES, LANES)

    squares = jnp.zeros((LANES, LANES), F32)
    traces = jnp.zeros((LANES, LANES), F32)
    diagonals = {}
    for h in range(2):
        b0, b1, b2, b3 = [(i + h) % 4 for i in range(4)]
        packed = half[h, 0:128, :]
        packed_t = packed.T
        spare = jnp.broadcast_to(half[h, 512:513, :], (LANES, LANES))
        diagonals[b0] = jnp.where(upper, packed, packed_t)
        diagonals[b2] = jnp.where(eye, spare, jnp.where(upper, packed_t, packed))
        for start, a, b in ((128, b0, b1), (256, b2, b3), (384, b0, b2)):
            block = half[h, start : start + LANES, :]
            squares = squares + 2.0 * (block * block)
            p_ref[block_at(a, b)] = block
            p_ref[block_at(b, a)] = block.T
    for block in diagonals.values():
        traces = traces + jnp.where(eye, block, 0.0)
    shift = damp_ref[chip] * jnp.sum(traces) / WIDTH
    for a, block in diagonals.items():
        block = block + jnp.where(eye, shift, 0.0)
        squares = squares + block * block
        p_ref[block_at(a, a)] = block
    scaled = jnp.full((8, LANES), jnp.sum(squares) + EPSILON, F32)
    unit = (1.0 / jnp.sqrt(scaled))[0:1, 0:1]
    p_ref[...] = p_ref[...] * unit
    cond[core, chip] = cond[core, chip] * unit

    def twice(a_high, a_low, b_high, b_low):
        both = dot(jnp.concatenate([a_high, a_low], axis=0), b_high)
        rows = a_high.shape[0]
        return both[:rows] + (both[rows:] + dot(a_high, b_low))

    def newton(step, carry):
        value = p_ref[...]
        vector = cond[core, chip]
        high, low_ = split(value)
        v_high, v_low = split(vector)
        left_hi = jnp.concatenate([high[:MID], v_high], axis=0)
        left_lo = jnp.concatenate([low_[:MID], v_low], axis=0)
        prod = twice(left_hi, left_lo, high, low_)
        corner = twice(high[MID:], low_[MID:], high[:, MID:], low_[:, MID:])
        upper_rows = 2.0 * value[:MID] - prod[:MID]
        p_ref[:MID, :] = upper_rows
        p_ref[MID:, :MID] = upper_rows[:, MID:].T
        p_ref[MID:, MID:] = 2.0 * value[MID:, MID:] - corner
        cond[core, chip] = 2.0 * vector - prod[MID:]
        return carry

    for step in range(NEWTON_STEPS - 2):
        newton(step, 0)
    high, low_ = split(p_ref[...])

    def apply(vector):
        v_high, v_low = split(vector)
        return twice(v_high, v_low, high, low_)

    vector = cond[core, chip]
    vector = 2.0 * vector - apply(vector)
    once = apply(vector)
    vector = 2.0 * vector - (2.0 * once - apply(once))
    cond[core, chip] = vector

    halves = (pl.ds(0, HALF_Q // 2), pl.ds(HALF_Q // 2, HALF_Q // 2))
    first_to = (dev(fst + 1, snd), dev(fst - 1, snd))
    second_to = (plus, minus)
    sent = []

    def at(a, b, rows=None):
        ref = cond.at[core, chip_at(wrap(fst + a), wrap(snd + b))]
        return ref if rows is None else ref.at[rows]

    def go(ref, place, device):
        c = copy(ref, ref, place, device)
        c.start()
        sent.append(c)

    def come(ref, place):
        copy(ref, ref, place, partner).wait_recv()

    def hand_over(a, b):
        go(at(a, b), PAR + a * 4 + b, partner)

    def both_ways(a, b, place, devices):
        for n in range(2):
            for way in range(2):
                h = n ^ way
                go(at(a, b, halves[h]), place + 2 * way + n, devices[way])

    def along_first(b):
        both_ways(0, b, FST + 6 * b, first_to)

    def pass_first(b):
        for way in range(2):
            come(at(3 - 2 * way, b, halves[way]), FST + 6 * b + 2 * way)
            go(at(3 - 2 * way, b, halves[way]), FST + 6 * b + 4 + way, first_to[way])

    def rest_first(b):
        for way in range(2):
            come(at(3 - 2 * way, b, halves[1 - way]), FST + 6 * b + 2 * way + 1)
            hand_over(3 - 2 * way, b)

    def far_first(b):
        for way in range(2):
            come(at(2, b, halves[way]), FST + 6 * b + 4 + way)
        hand_over(2, b)

    def score(c, j):
        left = jnp.concatenate(split(cond[c, j]), axis=0)
        got = dot_t(left, grads[j])
        got = got[:, :ROWS] + got[:, ROWS:]
        rows = pl.ds(pl.multiple_of(c * HALF_Q, HALF_Q), HALF_Q)
        acc[rows, :] = acc[rows, :] + (got[:HALF_Q] + got[HALF_Q:])

    def own(a, b):
        score(core, chip_at(wrap(fst + a), wrap(snd + b)))

    def other(a, b):
        c = 1 - core
        j = chip_at(wrap(snd + a), wrap(fst + b), c)
        come(cond.at[c, j], PAR + a * 4 + b)
        score(c, j)

    acc[...] = jnp.zeros((2 * HALF_Q, ROWS), F32)
    both_ways(0, 0, SEC, second_to)
    along_first(0)
    hand_over(0, 0)
    for way in range(2):
        come(at(0, 3 - 2 * way, halves[way]), SEC + 2 * way)
        go(at(0, 3 - 2 * way, halves[way]), SEC + 4 + way, second_to[way])
    for way in range(2):
        come(at(0, 3 - 2 * way, halves[1 - way]), SEC + 2 * way + 1)
        along_first(3 - 2 * way)
        hand_over(0, 3 - 2 * way)
    pass_first(0)
    rest_first(0)
    own(0, 0)
    for way in range(2):
        come(at(0, 2, halves[way]), SEC + 4 + way)
    along_first(2)
    hand_over(0, 2)
    own(0, 3)
    own(0, 1)
    other(0, 0)
    pass_first(3)
    rest_first(3)
    own(0, 2)
    own(3, 0)
    pass_first(1)
    rest_first(1)
    own(1, 0)
    other(0, 3)
    far_first(0)
    other(0, 1)
    pass_first(2)
    rest_first(2)
    own(3, 3)
    own(1, 3)
    other(3, 0)
    other(1, 0)
    far_first(3)
    own(3, 1)
    own(1, 1)
    other(0, 2)
    far_first(1)
    own(2, 0)
    for a, b in ((3, 2), (1, 2), (2, 3)):
        own(a, b)
    for a, b in ((3, 3), (1, 3), (3, 1)):
        other(a, b)
    far_first(2)
    own(2, 1)
    other(1, 1)
    other(2, 0)
    own(2, 2)
    for a, b in ((3, 2), (1, 2), (2, 3), (2, 1), (2, 2)):
        other(a, b)

    done = acc[...] * scale
    for h in range(2):
        zout[:, 8 * h : 8 * h + 8, :] = done[h * HALF_Q : (h + 1) * HALF_Q].reshape(DEPTH, 8, ROWS)

    def send_scores(i, carry):
        there = lax.rem(z + i, DEPTH)
        copy(zout.at[there], zin.at[i], ZED + i, (there, dp)).start()
        return carry

    lax.fori_loop(1, DEPTH, send_scores, 0)
    total = zout[z]
    for i in range(1, DEPTH):
        copy(zin.at[i], zin.at[i], ZED + i, partner).wait_recv()
        total = total + zin[i]
    out_ref[...] = jnp.concatenate([total[0:4], total[8:12], total[4:8], total[12:16]], axis=0)

    def sent_raw(k, carry):
        copy(stage.at[0], rx.at[0], RAW + k, partner).wait_send()
        return carry

    lax.fori_loop(0, CHIPS, sent_raw, 0)

    def sent_query(i, carry):
        copy(qstage.at[0], qrx.at[0], QRY + i, partner).wait_send()
        return carry

    lax.fori_loop(1, CHIPS, sent_query, 0)

    def sent_part(i, carry):
        copy(part.at[0], r2.at[0], R1 + i, partner).wait_send()
        return carry

    lax.fori_loop(0, 12, sent_part, 0)
    for c in (far_top, far_low, near_low, near_top, join_top, join_low, exchange, *sent):
        c.wait_send()

    def sent_scores(i, carry):
        copy(zout.at[0], zin.at[0], ZED + i, partner).wait_send()
        return carry

    lax.fori_loop(1, DEPTH, sent_scores, 0)


def per_device(train_grads, queries, damping):
    rows, modules, width = train_grads.shape
    total_rows = rows * lax.axis_size("dp")
    scale = 1.0 / math.sqrt(modules * lax.axis_size("mod") * width)
    vmem = pltpu.VMEM
    out = pl.pallas_call(
        functools.partial(kernel, total_rows, scale),
        out_shape=jax.ShapeDtypeStruct((16, ROWS), F32),
        in_specs=[
            pl.BlockSpec(memory_space=pl.ANY),
            pl.BlockSpec(memory_space=pl.ANY),
            pl.BlockSpec(memory_space=pltpu.SMEM),
        ],
        out_specs=pl.BlockSpec(memory_space=vmem),
        scratch_shapes=[
            vmem((4, ROWS * CHIPS, LANES), F32),
            vmem((4, 4 * CHIPS, LANES), F32),
            vmem((CHIPS, ROWS, WIDTH), F32),
            vmem((CHIPS, ROWS, WIDTH), F32),
            vmem((CHIPS, 16, LANES), F32),
            vmem((CHIPS, 16, LANES), F32),
            vmem((CHIPS, TRI, LANES), F32),
            vmem((4, TRI, LANES), F32),
            vmem((8, TRI, LANES), F32),
            vmem((TRI, LANES), F32),
            vmem((2, TRI, LANES), F32),
            vmem((2, TRI, LANES), F32),
            vmem((WIDTH, WIDTH), F32),
            vmem((2, CHIPS, HALF_Q, WIDTH), F32),
            vmem((CHIPS, 2 * ROWS, WIDTH), BF16),
            vmem((2 * HALF_Q, ROWS), F32),
            vmem((DEPTH, 16, ROWS), F32),
            vmem((DEPTH, 16, ROWS), F32),
            pltpu.SemaphoreType.DMA((8,)),
            pltpu.SemaphoreType.DMA((COPIES,)),
            pltpu.SemaphoreType.DMA((COPIES,)),
        ],
        compiler_params=pltpu.CompilerParams(
            collective_id=0, has_side_effects=True, vmem_limit_bytes=60 * 2**20
        ),
    )(train_grads.reshape(rows * modules, width), queries.reshape(-1, width), damping)
    return out.T


def solution(mesh):
    return jax.shard_map(
        per_device,
        mesh=mesh,
        in_specs=(P("dp", "mod", None), P("dp", "mod", None), P("mod")),
        out_specs=P("dp", "mod"),
        check_vma=False,
    )
```

```python
import functools
import math

import jax
import jax.numpy as jnp
from jax import lax
from jax.experimental import pallas as pl
from jax.experimental.pallas import tpu as pltpu
from jax.sharding import PartitionSpec as P

NEWTON_STEPS = 8
EPSILON = 1e-06

SIDE = 4
CHIPS = SIDE * SIDE
DEPTH = 8
WIDTH = 512
ROWS = 128
LANES = 128
MID = WIDTH // 2
TRI = 4 * LANES + 8
TOP = 264
HALF_Q = 64
BF16 = jnp.bfloat16
F32 = jnp.float32

RAW = 0
QRY = RAW + 16
R1 = QRY + 16
R2 = R1 + 4
R3 = R2 + 8
R4 = R3 + 2
EXC = R4 + 4
SEC = EXC + 1
FST = SEC + 6
PAR = FST + 24
PAR_LOW = PAR + 16
ZED = PAR_LOW + 4
COPIES = ZED + 8


def split(value):
    high = value.astype(BF16)
    return high, (value - high.astype(F32)).astype(BF16)


def dot(a, b):
    return jnp.dot(a, b, preferred_element_type=F32)


def dot_t(a, b):
    return lax.dot_general(a, b, (((1,), (1,)), ((), ())), preferred_element_type=F32)


def wrap(i):
    return lax.rem(i + 2 * SIDE, SIDE)


def kernel(
    total_rows,
    scale,
    x_hbm,
    q_hbm,
    damp_ref,
    out_ref,
    x,
    q_in,
    stage,
    rx,
    qstage,
    qrx,
    part,
    r1,
    r2,
    r3,
    r4,
    half,
    p_ref,
    cond,
    grads,
    acc,
    zout,
    zin,
    in_sem,
    send,
    recv,
):
    z = lax.axis_index("mod")
    dp = lax.axis_index("dp")
    core = lax.rem(dp, 2)
    chip = lax.div(dp, 2)
    cx = lax.div(chip, SIDE)
    cy = lax.rem(chip, SIDE)
    fst = cx * (1 - core) + cy * core
    snd = cy * (1 - core) + cx * core

    def chip_at(p, q, c=core):
        return (p * (1 - c) + q * c) * SIDE + q * (1 - c) + p * c

    def dev(p, q):
        return (z, chip_at(wrap(p), wrap(q)) * 2 + core)

    partner = (z, chip * 2 + 1 - core)

    def copy(src, dst, place, device):
        return pltpu.make_async_remote_copy(
            src_ref=src,
            dst_ref=dst,
            send_sem=send.at[place],
            recv_sem=recv.at[place],
            device_id=device,
            device_id_type=pl.DeviceIdType.MESH,
        )

    loads = []
    for lb in range(4):
        cols = pl.ds(lb * LANES, LANES)
        loads.append(pltpu.make_async_copy(x_hbm.at[:, cols], x.at[lb], in_sem.at[lb]))
        loads.append(pltpu.make_async_copy(q_hbm.at[:, cols], q_in.at[lb], in_sem.at[4 + lb]))
    for load in loads:
        load.start()

    barrier = pltpu.get_barrier_semaphore()

    def greet_chip(i, carry):
        there = lax.rem(chip + i, CHIPS)
        pl.semaphore_signal(
            barrier, inc=1, device_id=(z, there * 2 + core), device_id_type=pl.DeviceIdType.MESH
        )
        return carry

    lax.fori_loop(1, CHIPS, greet_chip, 0)

    def greet_layer(i, carry):
        pl.semaphore_signal(
            barrier, inc=1, device_id=(lax.rem(z + i, DEPTH), dp), device_id_type=pl.DeviceIdType.MESH
        )
        return carry

    lax.fori_loop(1, DEPTH, greet_layer, 0)
    pl.semaphore_signal(barrier, inc=1, device_id=partner, device_id_type=pl.DeviceIdType.MESH)
    def second_of(b):
        return lax.rem(2 + 3 * b + lax.div(b, 2) * (3 - 2 * lax.rem(b, 2)), SIDE)

    def order(k):
        is0 = lax.div(CHIPS - 1 - k, 12)
        is3 = lax.div(k, 12)
        i = (k - 4) * (1 - is0) * (1 - is3)
        first = is0 * 2 + (1 - is0 - is3) * (1 + 2 * lax.rem(i, 2))
        late = lax.div(i, 4)
        middle = late * lax.div(i, 2) + (1 - late) * (1 - lax.rem(lax.div(i + 1, 2), 2))
        b = (is0 + is3) * lax.rem(k, 4) + (1 - is0 - is3) * middle
        return first, b

    def module_of(k, c):
        first, b = order(k)
        p = cx * (1 - c) + cy * c
        q = cy * (1 - c) + cx * c
        return chip_at(lax.rem(p + first, SIDE), lax.rem(q + second_of(b), SIDE), c)

    for load in loads:
        load.wait()

    def stage_rows(k):
        j = module_of(k, 1 - core)
        for lb in range(4):
            stage[j, :, pl.ds(lb * LANES, LANES)] = x[lb, pl.ds(j, ROWS, stride=CHIPS), :]

    def stage_first(k, carry):
        stage_rows(k)
        return carry

    def stage_query(j, carry):
        for lb in range(4):
            qstage[j, pl.ds(lb * 4, 4), :] = q_in[lb, pl.ds(j, 4, stride=CHIPS), :]
        return carry

    lax.fori_loop(0, 4, stage_first, 0)
    lax.fori_loop(0, CHIPS, stage_query, 0)
    pl.semaphore_wait(barrier, CHIPS - 1 + DEPTH - 1 + 1)

    def send_raw(k, carry):
        j = module_of(k, 1 - core)
        copy(stage.at[j], rx.at[j], RAW + k, partner).start()
        return carry

    def stage_and_send(k, carry):
        stage_rows(k)
        return send_raw(k, carry)

    lax.fori_loop(0, 4, send_raw, 0)

    def send_query(i, carry):
        there = lax.rem(chip + i, CHIPS)
        copy(qstage.at[there], qrx.at[chip], QRY + i, (z, there * 2 + core)).start()
        return carry

    lax.fori_loop(1, CHIPS, send_query, 0)
    lax.fori_loop(4, CHIPS, stage_and_send, 0)
    qrx[chip] = qstage[chip]

    row_of = lax.broadcasted_iota(jnp.int32, (LANES, LANES), 0)
    col_of = lax.broadcasted_iota(jnp.int32, (LANES, LANES), 1)
    upper = row_of <= col_of
    eye = row_of == col_of

    def gram(k):
        j = module_of(k, core)
        copy(stage.at[j], rx.at[j], RAW + k, partner).wait_recv()
        blocks, highs, lows = [], [], []
        for lb in range(4):
            cols = pl.ds(pl.multiple_of(lax.rem(lb + core, 4) * LANES, LANES), LANES)
            block = jnp.concatenate([stage[j, :, cols], rx[j, :, cols]], axis=0)
            high, low = split(block)
            grads[j, :ROWS, cols] = high[:ROWS]
            grads[j, ROWS:, cols] = low[:ROWS]
            blocks.append(block)
            highs.append(high)
            lows.append(low)
        left = jnp.concatenate([blocks[0].T, blocks[2].T], axis=0)
        left_hi, left_lo = split(left)
        right_hi = jnp.concatenate(highs, axis=1)
        right_lo = jnp.concatenate(lows, axis=1)
        prod = dot(left_hi, right_hi) + (dot(left_hi, right_lo) + dot(left_lo, right_hi))
        first, second = prod[:LANES], prod[LANES:]
        one, two = first[:, :LANES], second[:, 2 * LANES : 3 * LANES]
        diagonal = jnp.sum(jnp.where(eye, two, 0.0), axis=0, keepdims=True)
        part[k, 0:128, :] = jnp.where(upper, one, two)
        part[k, 128:256, :] = first[:, LANES : 2 * LANES]
        part[k, 256:384, :] = second[:, 3 * LANES :]
        part[k, 384:512, :] = first[:, 2 * LANES : 3 * LANES]
        part[k, 512:520, :] = jnp.broadcast_to(diagonal, (8, LANES))

    def side(odd):
        return 1 - 2 * odd

    def far(i, carry):
        gram(i)
        copy(part.at[i], r1.at[i], R1 + i, dev(fst + side(lax.rem(i, 2)), snd)).start()
        return carry

    lax.fori_loop(0, 4, far, 0)

    def grams(low, high):
        def step(k, carry):
            gram(k)
            return carry

        lax.fori_loop(low, high, step, 0)

    def near(k, slot):
        copy(part.at[k], r2.at[slot], R2 + slot, dev(fst + (1 if slot < 4 else -1), snd)).start()

    def joined(k, i, slot):
        copy(part.at[i], r1.at[i], R1 + i, partner).wait_recv()
        part[k] = part[k] + r1[i]
        near(k, slot)

    grams(4, 5)
    near(4, 1)
    grams(5, 6)
    near(5, 4)
    grams(6, 12)
    joined(6, 0, 0)
    joined(7, 1, 5)
    near(9, 6)
    grams(12, 16)
    joined(8, 2, 2)
    near(10, 3)
    joined(11, 3, 7)

    def arrived(b):
        for s in (0, 4):
            copy(r2.at[s + b], r2.at[s + b], R2 + s + b, partner).wait_recv()
        part[12 + b] = part[12 + b] + r2[b] + r2[4 + b]

    def wait_query(i, carry):
        copy(qstage.at[i], qrx.at[i], QRY + i, partner).wait_recv()
        return carry

    lax.fori_loop(1, CHIPS, wait_query, 0)
    for lb in range(4):
        cond[core, chip, :, lb * LANES : (lb + 1) * LANES] = jnp.concatenate(
            [qrx[i, lb * 4 : lb * 4 + 4, :] for i in range(CHIPS)], axis=0
        )

    top = pl.ds(0, TOP)
    low = pl.ds(TOP, TRI - TOP)
    plus = dev(fst, snd + 1)
    minus = dev(fst, snd - 1)

    def second_copy(b, rows, into, place, device):
        return copy(part.at[12 + b, rows], into.at[rows], place, device)

    arrived(0)
    far_top = second_copy(0, top, r3, R3, plus)
    far_low = second_copy(0, low, r3, R3 + 1, minus)
    far_top.start()
    far_low.start()
    arrived(1)
    near_low = second_copy(1, low, r4.at[0], R4 + 1, plus)
    near_low.start()
    arrived(2)
    near_top = second_copy(2, top, r4.at[1], R4 + 2, minus)
    near_top.start()
    far_top.wait_recv()
    part[13, top] = part[13, top] + r3[top]
    join_top = second_copy(1, top, r4.at[0], R4, plus)
    join_top.start()
    far_low.wait_recv()
    part[14, low] = part[14, low] + r3[low]
    join_low = second_copy(2, low, r4.at[1], R4 + 3, minus)
    join_low.start()
    arrived(3)
    near_low.wait_recv()
    near_top.wait_recv()
    join_top.wait_recv()
    join_low.wait_recv()
    half[core] = (part[15] + r4[0] + r4[1]) * (1.0 / total_rows)
    exchange = copy(half.at[core], half.at[core], EXC, partner)
    exchange.start()

    copy(half.at[1 - core], half.at[1 - core], EXC, partner).wait_recv()

    def block_at(a, b):
        return pl.ds(a * LANES, LANES), pl.ds(b * LANES, LANES)

    squares = jnp.zeros((LANES, LANES), F32)
    traces = jnp.zeros((LANES, LANES), F32)
    diagonals = {}
    for h in range(2):
        b0, b1, b2, b3 = [(i + h) % 4 for i in range(4)]
        packed = half[h, 0:128, :]
        packed_t = packed.T
        spare = jnp.broadcast_to(half[h, 512:513, :], (LANES, LANES))
        diagonals[b0] = jnp.where(upper, packed, packed_t)
        diagonals[b2] = jnp.where(eye, spare, jnp.where(upper, packed_t, packed))
        for start, a, b in ((128, b0, b1), (256, b2, b3), (384, b0, b2)):
            block = half[h, start : start + LANES, :]
            squares = squares + 2.0 * (block * block)
            p_ref[block_at(a, b)] = block
            p_ref[block_at(b, a)] = block.T
    for block in diagonals.values():
        traces = traces + jnp.where(eye, block, 0.0)
    shift = damp_ref[chip] * jnp.sum(traces) / WIDTH
    for a, block in diagonals.items():
        block = block + jnp.where(eye, shift, 0.0)
        squares = squares + block * block
        p_ref[block_at(a, a)] = block
    scaled = jnp.full((8, LANES), jnp.sum(squares) + EPSILON, F32)
    unit = (1.0 / jnp.sqrt(scaled))[0:1, 0:1]
    p_ref[...] = p_ref[...] * unit
    cond[core, chip] = cond[core, chip] * unit

    def twice(a_high, a_low, b_high, b_low):
        both = dot(jnp.concatenate([a_high, a_low], axis=0), b_high)
        rows = a_high.shape[0]
        return both[:rows] + (both[rows:] + dot(a_high, b_low))

    def newton(step, carry):
        value = p_ref[...]
        vector = cond[core, chip]
        high, low_ = split(value)
        v_high, v_low = split(vector)
        left_hi = jnp.concatenate([high[:MID], v_high], axis=0)
        left_lo = jnp.concatenate([low_[:MID], v_low], axis=0)
        prod = twice(left_hi, left_lo, high, low_)
        corner = twice(high[MID:], low_[MID:], high[:, MID:], low_[:, MID:])
        upper_rows = 2.0 * value[:MID] - prod[:MID]
        p_ref[:MID, :] = upper_rows
        p_ref[MID:, :MID] = upper_rows[:, MID:].T
        p_ref[MID:, MID:] = 2.0 * value[MID:, MID:] - corner
        cond[core, chip] = 2.0 * vector - prod[MID:]
        return carry

    for step in range(NEWTON_STEPS - 2):
        newton(step, 0)
    high, low_ = split(p_ref[...])

    def apply(vector):
        v_high, v_low = split(vector)
        return twice(v_high, v_low, high, low_)

    vector = cond[core, chip]
    vector = 2.0 * vector - apply(vector)
    once = apply(vector)
    vector = 2.0 * vector - (2.0 * once - apply(once))
    cond[core, chip] = vector

    halves = (pl.ds(0, HALF_Q // 2), pl.ds(HALF_Q // 2, HALF_Q // 2))
    first_to = (dev(fst + 1, snd), dev(fst - 1, snd))
    second_to = (plus, minus)
    sent = []

    def at(a, b, rows=None):
        ref = cond.at[core, chip_at(wrap(fst + a), wrap(snd + b))]
        return ref if rows is None else ref.at[rows]

    def go(ref, place, device):
        c = copy(ref, ref, place, device)
        c.start()
        sent.append(c)

    def come(ref, place):
        copy(ref, ref, place, partner).wait_recv()

    def hand_over(a, b):
        go(at(a, b), PAR + a * 4 + b, partner)

    def both_ways(a, b, place, devices):
        for n in range(2):
            for way in range(2):
                h = n ^ way
                go(at(a, b, halves[h]), place + 2 * way + n, devices[way])

    def along_first(b):
        both_ways(0, b, FST + 6 * b, first_to)

    def pass_first(b):
        for way in range(2):
            come(at(3 - 2 * way, b, halves[way]), FST + 6 * b + 2 * way)
            go(at(3 - 2 * way, b, halves[way]), FST + 6 * b + 4 + way, first_to[way])

    def rest_first(b):
        for way in range(2):
            come(at(3 - 2 * way, b, halves[1 - way]), FST + 6 * b + 2 * way + 1)
            hand_over(3 - 2 * way, b)

    def far_first(b):
        for way in range(2):
            come(at(2, b, halves[way]), FST + 6 * b + 4 + way)
            go(at(2, b, halves[way]), PAR_LOW + b if way else PAR + 8 + b, partner)

    def score(c, j):
        left = jnp.concatenate(split(cond[c, j]), axis=0)
        got = dot_t(left, grads[j])
        got = got[:, :ROWS] + got[:, ROWS:]
        rows = pl.ds(pl.multiple_of(c * HALF_Q, HALF_Q), HALF_Q)
        acc[rows, :] = acc[rows, :] + (got[:HALF_Q] + got[HALF_Q:])

    def own(a, b):
        score(core, chip_at(wrap(fst + a), wrap(snd + b)))

    def other(a, b):
        c = 1 - core
        j = chip_at(wrap(snd + a), wrap(fst + b), c)
        if a == 2:
            come(cond.at[c, j, halves[0]], PAR + 8 + b)
            come(cond.at[c, j, halves[1]], PAR_LOW + b)
        else:
            come(cond.at[c, j], PAR + a * 4 + b)
        score(c, j)

    acc[...] = jnp.zeros((2 * HALF_Q, ROWS), F32)
    both_ways(0, 0, SEC, second_to)
    along_first(0)
    hand_over(0, 0)
    for way in range(2):
        come(at(0, 3 - 2 * way, halves[way]), SEC + 2 * way)
        go(at(0, 3 - 2 * way, halves[way]), SEC + 4 + way, second_to[way])
    pass_first(0)
    for way in range(2):
        come(at(0, 3 - 2 * way, halves[1 - way]), SEC + 2 * way + 1)
        along_first(3 - 2 * way)
        hand_over(0, 3 - 2 * way)
    rest_first(0)
    own(0, 0)
    for way in range(2):
        come(at(0, 2, halves[way]), SEC + 4 + way)
    along_first(2)
    hand_over(0, 2)
    own(0, 3)
    own(0, 1)
    other(0, 0)
    pass_first(3)
    rest_first(3)
    own(0, 2)
    own(3, 0)
    pass_first(1)
    rest_first(1)
    own(1, 0)
    other(0, 3)
    far_first(0)
    other(0, 1)
    pass_first(2)
    rest_first(2)
    own(3, 3)
    own(1, 3)
    other(3, 0)
    other(1, 0)
    far_first(3)
    own(3, 1)
    own(1, 1)
    other(0, 2)
    far_first(1)
    own(2, 0)
    for a, b in ((3, 2), (1, 2), (2, 3)):
        own(a, b)
    for a, b in ((3, 3), (1, 3), (3, 1)):
        other(a, b)
    far_first(2)
    own(2, 1)
    other(1, 1)
    other(2, 0)
    own(2, 2)
    for a, b in ((3, 2), (1, 2), (2, 3), (2, 1), (2, 2)):
        other(a, b)

    done = acc[...] * scale
    for h in range(2):
        zout[:, 8 * h : 8 * h + 8, :] = done[h * HALF_Q : (h + 1) * HALF_Q].reshape(DEPTH, 8, ROWS)

    def send_scores(i, carry):
        there = lax.rem(z + i, DEPTH)
        copy(zout.at[there], zin.at[i], ZED + i, (there, dp)).start()
        return carry

    lax.fori_loop(DEPTH // 2, DEPTH, send_scores, 0)
    lax.fori_loop(1, DEPTH // 2, send_scores, 0)
    def sent_raw(k, carry):
        copy(stage.at[0], rx.at[0], RAW + k, partner).wait_send()
        return carry

    lax.fori_loop(0, CHIPS, sent_raw, 0)

    def sent_query(i, carry):
        copy(qstage.at[0], qrx.at[0], QRY + i, partner).wait_send()
        return carry

    lax.fori_loop(1, CHIPS, sent_query, 0)

    def sent_part(i, carry):
        copy(part.at[0], r2.at[0], R1 + i, partner).wait_send()
        return carry

    lax.fori_loop(0, 12, sent_part, 0)
    for c in (far_top, far_low, near_low, near_top, join_top, join_low, exchange, *sent):
        c.wait_send()

    total = zout[z]
    for i in range(1, DEPTH):
        copy(zin.at[i], zin.at[i], ZED + i, partner).wait_recv()
        total = total + zin[i]
    out_ref[...] = jnp.concatenate([total[0:4], total[8:12], total[4:8], total[12:16]], axis=0)

    def sent_scores(i, carry):
        copy(zout.at[0], zin.at[0], ZED + i, partner).wait_send()
        return carry

    lax.fori_loop(1, DEPTH, sent_scores, 0)


def per_device(train_grads, queries, damping):
    rows, modules, width = train_grads.shape
    total_rows = rows * lax.axis_size("dp")
    scale = 1.0 / math.sqrt(modules * lax.axis_size("mod") * width)
    vmem = pltpu.VMEM
    out = pl.pallas_call(
        functools.partial(kernel, total_rows, scale),
        out_shape=jax.ShapeDtypeStruct((16, ROWS), F32),
        in_specs=[
            pl.BlockSpec(memory_space=pl.ANY),
            pl.BlockSpec(memory_space=pl.ANY),
            pl.BlockSpec(memory_space=pltpu.SMEM),
        ],
        out_specs=pl.BlockSpec(memory_space=vmem),
        scratch_shapes=[
            vmem((4, ROWS * CHIPS, LANES), F32),
            vmem((4, 4 * CHIPS, LANES), F32),
            vmem((CHIPS, ROWS, WIDTH), F32),
            vmem((CHIPS, ROWS, WIDTH), F32),
            vmem((CHIPS, 16, LANES), F32),
            vmem((CHIPS, 16, LANES), F32),
            vmem((CHIPS, TRI, LANES), F32),
            vmem((4, TRI, LANES), F32),
            vmem((8, TRI, LANES), F32),
            vmem((TRI, LANES), F32),
            vmem((2, TRI, LANES), F32),
            vmem((2, TRI, LANES), F32),
            vmem((WIDTH, WIDTH), F32),
            vmem((2, CHIPS, HALF_Q, WIDTH), F32),
            vmem((CHIPS, 2 * ROWS, WIDTH), BF16),
            vmem((2 * HALF_Q, ROWS), F32),
            vmem((DEPTH, 16, ROWS), F32),
            vmem((DEPTH, 16, ROWS), F32),
            pltpu.SemaphoreType.DMA((8,)),
            pltpu.SemaphoreType.DMA((COPIES,)),
            pltpu.SemaphoreType.DMA((COPIES,)),
        ],
        compiler_params=pltpu.CompilerParams(
            collective_id=0, has_side_effects=True, vmem_limit_bytes=60 * 2**20
        ),
    )(train_grads.reshape(rows * modules, width), queries.reshape(-1, width), damping)
    return out.T


def solution(mesh):
    return jax.shard_map(
        per_device,
        mesh=mesh,
        in_specs=(P("dp", "mod", None), P("dp", "mod", None), P("mod")),
        out_specs=P("dp", "mod"),
        check_vma=False,
    )
```

```python
import functools
import math

import jax
import jax.numpy as jnp
from jax import lax
from jax.experimental import pallas as pl
from jax.experimental.pallas import tpu as pltpu
from jax.sharding import PartitionSpec as P

NEWTON_STEPS = 8
EPSILON = 1e-06

SIDE = 4
CHIPS = SIDE * SIDE
DEPTH = 8
WIDTH = 512
ROWS = 128
LANES = 128
MID = WIDTH // 2
TRI = 4 * LANES + 8
TOP = 264
HALF_Q = 64
BF16 = jnp.bfloat16
F32 = jnp.float32

RAW = 0
QRY = RAW + 16
R1 = QRY + 16
R2 = R1 + 8
R3 = R2 + 16
R4 = R3 + 2
EXC = R4 + 2
SEC = EXC + 1
FST = SEC + 6
PAR = FST + 24
PAR_LOW = PAR + 16
ZED = PAR_LOW + 4
COPIES = ZED + 8


def split(value):
    high = value.astype(BF16)
    return high, (value - high.astype(F32)).astype(BF16)


def dot(a, b):
    return jnp.dot(a, b, preferred_element_type=F32)


def dot_t(a, b):
    return lax.dot_general(a, b, (((1,), (1,)), ((), ())), preferred_element_type=F32)


def wrap(i):
    return lax.rem(i + 2 * SIDE, SIDE)


def kernel(
    total_rows,
    scale,
    x_hbm,
    q_hbm,
    damp_ref,
    out_ref,
    x,
    q_in,
    stage,
    rx,
    qstage,
    qrx,
    part,
    r1,
    r2,
    r3,
    r4,
    half,
    p_ref,
    cond,
    grads,
    acc,
    zout,
    zin,
    in_sem,
    send,
    recv,
):
    z = lax.axis_index("mod")
    dp = lax.axis_index("dp")
    core = lax.rem(dp, 2)
    chip = lax.div(dp, 2)
    cx = lax.div(chip, SIDE)
    cy = lax.rem(chip, SIDE)
    fst = cx * (1 - core) + cy * core
    snd = cy * (1 - core) + cx * core

    def chip_at(p, q, c=core):
        return (p * (1 - c) + q * c) * SIDE + q * (1 - c) + p * c

    def dev(p, q):
        return (z, chip_at(wrap(p), wrap(q)) * 2 + core)

    partner = (z, chip * 2 + 1 - core)

    def copy(src, dst, place, device):
        return pltpu.make_async_remote_copy(
            src_ref=src,
            dst_ref=dst,
            send_sem=send.at[place],
            recv_sem=recv.at[place],
            device_id=device,
            device_id_type=pl.DeviceIdType.MESH,
        )

    loads = []
    for lb in range(4):
        cols = pl.ds(lb * LANES, LANES)
        loads.append(pltpu.make_async_copy(x_hbm.at[:, cols], x.at[lb], in_sem.at[lb]))
        loads.append(pltpu.make_async_copy(q_hbm.at[:, cols], q_in.at[lb], in_sem.at[4 + lb]))
    for load in loads:
        load.start()

    barrier = pltpu.get_barrier_semaphore()

    def greet_chip(i, carry):
        there = lax.rem(chip + i, CHIPS)
        pl.semaphore_signal(
            barrier, inc=1, device_id=(z, there * 2 + core), device_id_type=pl.DeviceIdType.MESH
        )
        return carry

    lax.fori_loop(1, CHIPS, greet_chip, 0)

    def greet_layer(i, carry):
        pl.semaphore_signal(
            barrier, inc=1, device_id=(lax.rem(z + i, DEPTH), dp), device_id_type=pl.DeviceIdType.MESH
        )
        return carry

    lax.fori_loop(1, DEPTH, greet_layer, 0)
    pl.semaphore_signal(barrier, inc=1, device_id=partner, device_id_type=pl.DeviceIdType.MESH)
    def second_of(b):
        return lax.rem(2 + 3 * b + lax.div(b, 2) * (3 - 2 * lax.rem(b, 2)), SIDE)

    def order(k):
        is0 = lax.div(CHIPS - 1 - k, 12)
        is3 = lax.div(k, 12)
        near = 1 - is0 - is3
        first = is0 * 2 + near * (1 + 2 * lax.rem(k, 2))
        b = (is0 + is3) * lax.rem(k, 4) + near * lax.div(k - 4, 2)
        return first, b

    def module_of(k, c):
        first, b = order(k)
        p = cx * (1 - c) + cy * c
        q = cy * (1 - c) + cx * c
        return chip_at(lax.rem(p + first, SIDE), lax.rem(q + second_of(b), SIDE), c)

    for load in loads:
        load.wait()

    def stage_rows(k):
        j = module_of(k, 1 - core)
        for lb in range(4):
            stage[j, :, pl.ds(lb * LANES, LANES)] = x[lb, pl.ds(j, ROWS, stride=CHIPS), :]

    def stage_first(k, carry):
        stage_rows(k)
        return carry

    def stage_query(j, carry):
        for lb in range(4):
            qstage[j, pl.ds(lb * 4, 4), :] = q_in[lb, pl.ds(j, 4, stride=CHIPS), :]
        return carry

    lax.fori_loop(0, 4, stage_first, 0)
    lax.fori_loop(0, CHIPS, stage_query, 0)
    pl.semaphore_wait(barrier, CHIPS - 1 + DEPTH - 1 + 1)

    def send_raw(k, carry):
        j = module_of(k, 1 - core)
        copy(stage.at[j], rx.at[j], RAW + k, partner).start()
        return carry

    def stage_and_send(k, carry):
        stage_rows(k)
        return send_raw(k, carry)

    lax.fori_loop(0, 4, send_raw, 0)

    def send_query(i, carry):
        there = lax.rem(chip + i, CHIPS)
        copy(qstage.at[there], qrx.at[chip], QRY + i, (z, there * 2 + core)).start()
        return carry

    lax.fori_loop(1, CHIPS, send_query, 0)
    lax.fori_loop(4, CHIPS, stage_and_send, 0)
    qrx[chip] = qstage[chip]

    row_of = lax.broadcasted_iota(jnp.int32, (LANES, LANES), 0)
    col_of = lax.broadcasted_iota(jnp.int32, (LANES, LANES), 1)
    upper = row_of <= col_of
    eye = row_of == col_of

    def gram(k):
        j = module_of(k, core)
        copy(stage.at[j], rx.at[j], RAW + k, partner).wait_recv()
        blocks, highs, lows = [], [], []
        for lb in range(4):
            cols = pl.ds(pl.multiple_of(lax.rem(lb + core, 4) * LANES, LANES), LANES)
            block = jnp.concatenate([stage[j, :, cols], rx[j, :, cols]], axis=0)
            high, low = split(block)
            grads[j, :ROWS, cols] = high[:ROWS]
            grads[j, ROWS:, cols] = low[:ROWS]
            blocks.append(block)
            highs.append(high)
            lows.append(low)
        left = jnp.concatenate([blocks[0].T, blocks[2].T], axis=0)
        left_hi, left_lo = split(left)
        right_hi = jnp.concatenate(highs, axis=1)
        right_lo = jnp.concatenate(lows, axis=1)
        prod = dot(left_hi, right_hi) + (dot(left_hi, right_lo) + dot(left_lo, right_hi))
        first, second = prod[:LANES], prod[LANES:]
        one, two = first[:, :LANES], second[:, 2 * LANES : 3 * LANES]
        diagonal = jnp.sum(jnp.where(eye, two, 0.0), axis=0, keepdims=True)
        part[k, 0:128, :] = jnp.where(upper, one, two)
        part[k, 128:256, :] = first[:, LANES : 2 * LANES]
        part[k, 256:384, :] = second[:, 3 * LANES :]
        part[k, 384:512, :] = first[:, 2 * LANES : 3 * LANES]
        part[k, 512:520, :] = jnp.broadcast_to(diagonal, (8, LANES))

    def grams(low, high):
        def step(k, carry):
            gram(k)
            return carry

        lax.fori_loop(low, high, step, 0)

    halves = (pl.ds(0, TOP), pl.ds(TOP, TRI - TOP))
    first_to = (dev(fst + 1, snd), dev(fst - 1, snd))

    def ring(src, dst, h, place, way):
        c = copy(src.at[halves[h]], dst.at[halves[h]], place, first_to[way])
        c.start()
        sent.append(c)

    sent = []

    def far(b):
        for way in range(2):
            ring(part.at[b], r1.at[b], way, R1 + 2 * b + way, way)

    def near(b, way, h):
        slot = 4 * way + b
        ring(part.at[4 + 2 * b + way], r2.at[slot], h, R2 + 2 * slot + h, way)

    def plain(b):
        for way in range(2):
            near(b, way, 1 - way)

    def joined(b):
        for way in range(2):
            k, rows = 4 + 2 * b + way, halves[way]
            copy(part.at[b, rows], r1.at[b, rows], R1 + 2 * b + way, partner).wait_recv()
            part[k, rows] = part[k, rows] + r1[b, rows]
            near(b, way, way)

    for b in range(3):
        grams(b, b + 1)
        far(b)
    grams(4, 6)
    plain(0)
    grams(3, 4)
    grams(6, 10)
    joined(0)
    far(3)
    plain(1)
    grams(10, 16)
    joined(1)
    plain(2)
    joined(2)
    plain(3)
    joined(3)

    def arrived(b):
        for slot in (b, 4 + b):
            for h, rows in enumerate(halves):
                copy(r2.at[slot, rows], r2.at[slot, rows], R2 + 2 * slot + h, partner).wait_recv()
        part[12 + b] = part[12 + b] + r2[b] + r2[4 + b]

    def wait_query(i, carry):
        copy(qstage.at[i], qrx.at[i], QRY + i, partner).wait_recv()
        return carry

    lax.fori_loop(1, CHIPS, wait_query, 0)
    for lb in range(4):
        cond[core, chip, :, lb * LANES : (lb + 1) * LANES] = jnp.concatenate(
            [qrx[i, lb * 4 : lb * 4 + 4, :] for i in range(CHIPS)], axis=0
        )

    second_to = (dev(fst, snd + 1), dev(fst, snd - 1))
    arrived(0)
    over = []
    for way, rows in enumerate(halves):
        over.append(copy(part.at[12, rows], r3.at[rows], R3 + way, second_to[way]))
        over[-1].start()
    onto = []
    for way, rows in enumerate(halves):
        arrived(1 + way)
        over[way].wait_recv()
        part[13 + way, rows] = part[13 + way, rows] + r3[rows]
        onto.append(copy(part.at[13 + way], r4.at[way], R4 + way, second_to[way]))
        onto[-1].start()
    arrived(3)
    for c in onto:
        c.wait_recv()
    half[core] = (part[15] + r4[0] + r4[1]) * (1.0 / total_rows)
    exchange = copy(half.at[core], half.at[core], EXC, partner)
    exchange.start()

    copy(half.at[1 - core], half.at[1 - core], EXC, partner).wait_recv()

    def block_at(a, b):
        return pl.ds(a * LANES, LANES), pl.ds(b * LANES, LANES)

    squares = jnp.zeros((LANES, LANES), F32)
    traces = jnp.zeros((LANES, LANES), F32)
    diagonals = {}
    for h in range(2):
        b0, b1, b2, b3 = [(i + h) % 4 for i in range(4)]
        packed = half[h, 0:128, :]
        packed_t = packed.T
        spare = jnp.broadcast_to(half[h, 512:513, :], (LANES, LANES))
        diagonals[b0] = jnp.where(upper, packed, packed_t)
        diagonals[b2] = jnp.where(eye, spare, jnp.where(upper, packed_t, packed))
        for start, a, b in ((128, b0, b1), (256, b2, b3), (384, b0, b2)):
            block = half[h, start : start + LANES, :]
            squares = squares + 2.0 * (block * block)
            p_ref[block_at(a, b)] = block
            p_ref[block_at(b, a)] = block.T
    for block in diagonals.values():
        traces = traces + jnp.where(eye, block, 0.0)
    shift = damp_ref[chip] * jnp.sum(traces) / WIDTH
    for a, block in diagonals.items():
        block = block + jnp.where(eye, shift, 0.0)
        squares = squares + block * block
        p_ref[block_at(a, a)] = block
    scaled = jnp.full((8, LANES), jnp.sum(squares) + EPSILON, F32)
    unit = (1.0 / jnp.sqrt(scaled))[0:1, 0:1]
    p_ref[...] = p_ref[...] * unit
    cond[core, chip] = cond[core, chip] * unit

    def twice(a_high, a_low, b_high, b_low):
        both = dot(jnp.concatenate([a_high, a_low], axis=0), b_high)
        rows = a_high.shape[0]
        return both[:rows] + (both[rows:] + dot(a_high, b_low))

    def newton(step, carry):
        value = p_ref[...]
        vector = cond[core, chip]
        high, low_ = split(value)
        v_high, v_low = split(vector)
        left_hi = jnp.concatenate([high[:MID], v_high], axis=0)
        left_lo = jnp.concatenate([low_[:MID], v_low], axis=0)
        prod = twice(left_hi, left_lo, high, low_)
        corner = twice(high[MID:], low_[MID:], high[:, MID:], low_[:, MID:])
        upper_rows = 2.0 * value[:MID] - prod[:MID]
        p_ref[:MID, :] = upper_rows
        p_ref[MID:, :MID] = upper_rows[:, MID:].T
        p_ref[MID:, MID:] = 2.0 * value[MID:, MID:] - corner
        cond[core, chip] = 2.0 * vector - prod[MID:]
        return carry

    for step in range(NEWTON_STEPS - 2):
        newton(step, 0)
    high, low_ = split(p_ref[...])

    def apply(vector):
        v_high, v_low = split(vector)
        return twice(v_high, v_low, high, low_)

    vector = cond[core, chip]
    vector = 2.0 * vector - apply(vector)
    once = apply(vector)
    vector = 2.0 * vector - (2.0 * once - apply(once))
    cond[core, chip] = vector

    halves = (pl.ds(0, HALF_Q // 2), pl.ds(HALF_Q // 2, HALF_Q // 2))

    def at(a, b, rows=None):
        ref = cond.at[core, chip_at(wrap(fst + a), wrap(snd + b))]
        return ref if rows is None else ref.at[rows]

    def go(ref, place, device):
        c = copy(ref, ref, place, device)
        c.start()
        sent.append(c)

    def come(ref, place):
        copy(ref, ref, place, partner).wait_recv()

    def hand_over(a, b):
        go(at(a, b), PAR + a * 4 + b, partner)

    def both_ways(a, b, place, devices):
        for n in range(2):
            for way in range(2):
                h = n ^ way
                go(at(a, b, halves[h]), place + 2 * way + n, devices[way])

    def along_first(b):
        both_ways(0, b, FST + 6 * b, first_to)

    def pass_first(b):
        for way in range(2):
            come(at(3 - 2 * way, b, halves[way]), FST + 6 * b + 2 * way)
            go(at(3 - 2 * way, b, halves[way]), FST + 6 * b + 4 + way, first_to[way])

    def rest_first(b):
        for way in range(2):
            come(at(3 - 2 * way, b, halves[1 - way]), FST + 6 * b + 2 * way + 1)
            hand_over(3 - 2 * way, b)

    def far_first(b):
        for way in range(2):
            come(at(2, b, halves[way]), FST + 6 * b + 4 + way)
            go(at(2, b, halves[way]), PAR_LOW + b if way else PAR + 8 + b, partner)

    def score(c, j):
        left = jnp.concatenate(split(cond[c, j]), axis=0)
        got = dot_t(left, grads[j])
        got = got[:, :ROWS] + got[:, ROWS:]
        rows = pl.ds(pl.multiple_of(c * HALF_Q, HALF_Q), HALF_Q)
        acc[rows, :] = acc[rows, :] + (got[:HALF_Q] + got[HALF_Q:])

    def own(a, b):
        score(core, chip_at(wrap(fst + a), wrap(snd + b)))

    def other(a, b):
        c = 1 - core
        j = chip_at(wrap(snd + a), wrap(fst + b), c)
        if a == 2:
            come(cond.at[c, j, halves[0]], PAR + 8 + b)
            come(cond.at[c, j, halves[1]], PAR_LOW + b)
        else:
            come(cond.at[c, j], PAR + a * 4 + b)
        score(c, j)

    acc[...] = jnp.zeros((2 * HALF_Q, ROWS), F32)
    both_ways(0, 0, SEC, second_to)
    along_first(0)
    hand_over(0, 0)
    for way in range(2):
        come(at(0, 3 - 2 * way, halves[way]), SEC + 2 * way)
        go(at(0, 3 - 2 * way, halves[way]), SEC + 4 + way, second_to[way])
    pass_first(0)
    for way in range(2):
        come(at(0, 3 - 2 * way, halves[1 - way]), SEC + 2 * way + 1)
        along_first(3 - 2 * way)
        hand_over(0, 3 - 2 * way)
    rest_first(0)
    own(0, 0)
    for way in range(2):
        come(at(0, 2, halves[way]), SEC + 4 + way)
    along_first(2)
    hand_over(0, 2)
    own(0, 3)
    own(0, 1)
    other(0, 0)
    pass_first(3)
    rest_first(3)
    own(0, 2)
    own(3, 0)
    pass_first(1)
    rest_first(1)
    own(1, 0)
    other(0, 3)
    far_first(0)
    other(0, 1)
    pass_first(2)
    rest_first(2)
    own(3, 3)
    own(1, 3)
    other(3, 0)
    other(1, 0)
    far_first(3)
    own(3, 1)
    own(1, 1)
    other(0, 2)
    far_first(1)
    own(2, 0)
    for a, b in ((3, 2), (1, 2), (2, 3)):
        own(a, b)
    for a, b in ((3, 3), (1, 3), (3, 1)):
        other(a, b)
    far_first(2)
    own(2, 1)
    other(1, 1)
    other(2, 0)
    own(2, 2)
    for a, b in ((3, 2), (1, 2), (2, 3), (2, 1), (2, 2)):
        other(a, b)

    done = acc[...] * scale
    for h in range(2):
        zout[:, 8 * h : 8 * h + 8, :] = done[h * HALF_Q : (h + 1) * HALF_Q].reshape(DEPTH, 8, ROWS)

    def send_scores(i, carry):
        there = lax.rem(z + i, DEPTH)
        copy(zout.at[there], zin.at[i], ZED + i, (there, dp)).start()
        return carry

    lax.fori_loop(DEPTH // 2, DEPTH, send_scores, 0)
    lax.fori_loop(1, DEPTH // 2, send_scores, 0)
    def sent_raw(k, carry):
        copy(stage.at[0], rx.at[0], RAW + k, partner).wait_send()
        return carry

    lax.fori_loop(0, CHIPS, sent_raw, 0)

    def sent_query(i, carry):
        copy(qstage.at[0], qrx.at[0], QRY + i, partner).wait_send()
        return carry

    lax.fori_loop(1, CHIPS, sent_query, 0)

    for c in (*over, *onto, exchange, *sent):
        c.wait_send()

    total = zout[z]
    for i in range(1, DEPTH):
        copy(zin.at[i], zin.at[i], ZED + i, partner).wait_recv()
        total = total + zin[i]
    out_ref[...] = jnp.concatenate([total[0:4], total[8:12], total[4:8], total[12:16]], axis=0)

    def sent_scores(i, carry):
        copy(zout.at[0], zin.at[0], ZED + i, partner).wait_send()
        return carry

    lax.fori_loop(1, DEPTH, sent_scores, 0)


def per_device(train_grads, queries, damping):
    rows, modules, width = train_grads.shape
    total_rows = rows * lax.axis_size("dp")
    scale = 1.0 / math.sqrt(modules * lax.axis_size("mod") * width)
    vmem = pltpu.VMEM
    out = pl.pallas_call(
        functools.partial(kernel, total_rows, scale),
        out_shape=jax.ShapeDtypeStruct((16, ROWS), F32),
        in_specs=[
            pl.BlockSpec(memory_space=pl.ANY),
            pl.BlockSpec(memory_space=pl.ANY),
            pl.BlockSpec(memory_space=pltpu.SMEM),
        ],
        out_specs=pl.BlockSpec(memory_space=vmem),
        scratch_shapes=[
            vmem((4, ROWS * CHIPS, LANES), F32),
            vmem((4, 4 * CHIPS, LANES), F32),
            vmem((CHIPS, ROWS, WIDTH), F32),
            vmem((CHIPS, ROWS, WIDTH), F32),
            vmem((CHIPS, 16, LANES), F32),
            vmem((CHIPS, 16, LANES), F32),
            vmem((CHIPS, TRI, LANES), F32),
            vmem((4, TRI, LANES), F32),
            vmem((8, TRI, LANES), F32),
            vmem((TRI, LANES), F32),
            vmem((2, TRI, LANES), F32),
            vmem((2, TRI, LANES), F32),
            vmem((WIDTH, WIDTH), F32),
            vmem((2, CHIPS, HALF_Q, WIDTH), F32),
            vmem((CHIPS, 2 * ROWS, WIDTH), BF16),
            vmem((2 * HALF_Q, ROWS), F32),
            vmem((DEPTH, 16, ROWS), F32),
            vmem((DEPTH, 16, ROWS), F32),
            pltpu.SemaphoreType.DMA((8,)),
            pltpu.SemaphoreType.DMA((COPIES,)),
            pltpu.SemaphoreType.DMA((COPIES,)),
        ],
        compiler_params=pltpu.CompilerParams(
            collective_id=0, has_side_effects=True, vmem_limit_bytes=60 * 2**20
        ),
    )(train_grads.reshape(rows * modules, width), queries.reshape(-1, width), damping)
    return out.T


def solution(mesh):
    return jax.shard_map(
        per_device,
        mesh=mesh,
        in_specs=(P("dp", "mod", None), P("dp", "mod", None), P("mod")),
        out_specs=P("dp", "mod"),
        check_vma=False,
    )
```

```python
import functools
import math

import jax
import jax.numpy as jnp
from jax import lax
from jax.experimental import pallas as pl
from jax.experimental.pallas import tpu as pltpu
from jax.sharding import PartitionSpec as P

NEWTON_STEPS = 8
EPSILON = 1e-06

SIDE = 4
CHIPS = SIDE * SIDE
DEPTH = 8
WIDTH = 512
ROWS = 128
LANES = 128
MID = WIDTH // 2
TRI = 4 * LANES + 8
TOP = 264
HALF_Q = 64
BF16 = jnp.bfloat16
F32 = jnp.float32

RAW = 0
QRY = RAW + 16
R1 = QRY + 16
R2 = R1 + 8
R3 = R2 + 16
R4 = R3 + 2
EXC = R4 + 2
SEC = EXC + 1
FST = SEC + 6
PAR = FST + 24
PAR_LOW = PAR + 16
ZED = PAR_LOW + 4
COPIES = ZED + 8


def split(value):
    high = value.astype(BF16)
    return high, (value - high.astype(F32)).astype(BF16)


def dot(a, b):
    return jnp.dot(a, b, preferred_element_type=F32)


def dot_t(a, b):
    return lax.dot_general(a, b, (((1,), (1,)), ((), ())), preferred_element_type=F32)


def wrap(i):
    return lax.rem(i + 2 * SIDE, SIDE)


def kernel(
    total_rows,
    scale,
    x_hbm,
    q_hbm,
    damp_ref,
    out_ref,
    x,
    q_in,
    stage,
    rx,
    qstage,
    qrx,
    part,
    r1,
    r2,
    r3,
    r4,
    half,
    p_ref,
    cond,
    grads,
    acc,
    zout,
    zin,
    in_sem,
    send,
    recv,
):
    z = lax.axis_index("mod")
    dp = lax.axis_index("dp")
    core = lax.rem(dp, 2)
    chip = lax.div(dp, 2)
    cx = lax.div(chip, SIDE)
    cy = lax.rem(chip, SIDE)
    fst = cx * (1 - core) + cy * core
    snd = cy * (1 - core) + cx * core

    def chip_at(p, q, c=core):
        return (p * (1 - c) + q * c) * SIDE + q * (1 - c) + p * c

    def dev(p, q):
        return (z, chip_at(wrap(p), wrap(q)) * 2 + core)

    partner = (z, chip * 2 + 1 - core)

    def copy(src, dst, place, device):
        return pltpu.make_async_remote_copy(
            src_ref=src,
            dst_ref=dst,
            send_sem=send.at[place],
            recv_sem=recv.at[place],
            device_id=device,
            device_id_type=pl.DeviceIdType.MESH,
        )

    loads = []
    for lb in range(4):
        cols = pl.ds(lb * LANES, LANES)
        loads.append(pltpu.make_async_copy(x_hbm.at[:, cols], x.at[lb], in_sem.at[lb]))
        loads.append(pltpu.make_async_copy(q_hbm.at[:, cols], q_in.at[lb], in_sem.at[4 + lb]))
    for load in loads:
        load.start()

    barrier = pltpu.get_barrier_semaphore()

    def greet_chip(i, carry):
        there = lax.rem(chip + i, CHIPS)
        pl.semaphore_signal(
            barrier, inc=1, device_id=(z, there * 2 + core), device_id_type=pl.DeviceIdType.MESH
        )
        return carry

    lax.fori_loop(1, CHIPS, greet_chip, 0)

    def greet_layer(i, carry):
        pl.semaphore_signal(
            barrier, inc=1, device_id=(lax.rem(z + i, DEPTH), dp), device_id_type=pl.DeviceIdType.MESH
        )
        return carry

    lax.fori_loop(1, DEPTH, greet_layer, 0)
    pl.semaphore_signal(barrier, inc=1, device_id=partner, device_id_type=pl.DeviceIdType.MESH)
    def second_of(b):
        return lax.rem(2 + 3 * b + lax.div(b, 2) * (3 - 2 * lax.rem(b, 2)), SIDE)

    def order(k):
        is0 = lax.div(CHIPS - 1 - k, 12)
        is3 = lax.div(k, 12)
        near = 1 - is0 - is3
        first = is0 * 2 + near * (1 + 2 * lax.rem(k, 2))
        b = (is0 + is3) * lax.rem(k, 4) + near * lax.div(k - 4, 2)
        return first, b

    def module_of(k, c):
        first, b = order(k)
        p = cx * (1 - c) + cy * c
        q = cy * (1 - c) + cx * c
        return chip_at(lax.rem(p + first, SIDE), lax.rem(q + second_of(b), SIDE), c)

    for load in loads:
        load.wait()

    def stage_rows(k):
        j = module_of(k, 1 - core)
        for lb in range(4):
            stage[j, :, pl.ds(lb * LANES, LANES)] = x[lb, pl.ds(j, ROWS, stride=CHIPS), :]

    def stage_first(k, carry):
        stage_rows(k)
        return carry

    def stage_query(j, carry):
        for lb in range(4):
            qstage[j, pl.ds(lb * 4, 4), :] = q_in[lb, pl.ds(j, 4, stride=CHIPS), :]
        return carry

    lax.fori_loop(0, 4, stage_first, 0)
    lax.fori_loop(0, CHIPS, stage_query, 0)
    pl.semaphore_wait(barrier, CHIPS - 1 + DEPTH - 1 + 1)

    def send_raw(k, carry):
        j = module_of(k, 1 - core)
        copy(stage.at[j], rx.at[j], RAW + k, partner).start()
        return carry

    def stage_and_send(k, carry):
        stage_rows(k)
        return send_raw(k, carry)


    def send_query(i, carry):
        there = lax.rem(chip + i, CHIPS)
        copy(qstage.at[there], qrx.at[chip], QRY + i, (z, there * 2 + core)).start()
        return carry

    lax.fori_loop(1, CHIPS, send_query, 0)
    lax.fori_loop(0, 4, send_raw, 0)
    lax.fori_loop(4, CHIPS, stage_and_send, 0)
    qrx[chip] = qstage[chip]

    row_of = lax.broadcasted_iota(jnp.int32, (LANES, LANES), 0)
    col_of = lax.broadcasted_iota(jnp.int32, (LANES, LANES), 1)
    upper = row_of <= col_of
    eye = row_of == col_of

    def gram(k):
        j = module_of(k, core)
        copy(stage.at[j], rx.at[j], RAW + k, partner).wait_recv()
        blocks, highs, lows = [], [], []
        for lb in range(4):
            cols = pl.ds(pl.multiple_of(lax.rem(lb + core, 4) * LANES, LANES), LANES)
            block = jnp.concatenate([stage[j, :, cols], rx[j, :, cols]], axis=0)
            high, low = split(block)
            grads[j, :ROWS, cols] = high[:ROWS]
            grads[j, ROWS:, cols] = low[:ROWS]
            blocks.append(block)
            highs.append(high)
            lows.append(low)
        left = jnp.concatenate([blocks[0].T, blocks[2].T], axis=0)
        left_hi, left_lo = split(left)
        right_hi = jnp.concatenate(highs, axis=1)
        right_lo = jnp.concatenate(lows, axis=1)
        prod = dot(left_hi, right_hi) + (dot(left_hi, right_lo) + dot(left_lo, right_hi))
        first, second = prod[:LANES], prod[LANES:]
        one, two = first[:, :LANES], second[:, 2 * LANES : 3 * LANES]
        diagonal = jnp.sum(jnp.where(eye, two, 0.0), axis=0, keepdims=True)
        part[k, 0:128, :] = jnp.where(upper, one, two)
        part[k, 128:256, :] = first[:, LANES : 2 * LANES]
        part[k, 256:384, :] = second[:, 3 * LANES :]
        part[k, 384:512, :] = first[:, 2 * LANES : 3 * LANES]
        part[k, 512:520, :] = jnp.broadcast_to(diagonal, (8, LANES))

    def grams(low, high):
        def step(k, carry):
            gram(k)
            return carry

        lax.fori_loop(low, high, step, 0)

    halves = (pl.ds(0, TOP), pl.ds(TOP, TRI - TOP))
    first_to = (dev(fst + 1, snd), dev(fst - 1, snd))

    def ring(src, dst, h, place, way):
        c = copy(src.at[halves[h]], dst.at[halves[h]], place, first_to[way])
        c.start()
        sent.append(c)

    sent = []

    def far(b):
        for way in range(2):
            ring(part.at[b], r1.at[b], way, R1 + 2 * b + way, way)

    def near(b, way, h):
        slot = 4 * way + b
        ring(part.at[4 + 2 * b + way], r2.at[slot], h, R2 + 2 * slot + h, way)

    def plain(b):
        for way in range(2):
            near(b, way, 1 - way)

    def joined(b):
        for way in range(2):
            k, rows = 4 + 2 * b + way, halves[way]
            copy(part.at[b, rows], r1.at[b, rows], R1 + 2 * b + way, partner).wait_recv()
            part[k, rows] = part[k, rows] + r1[b, rows]
            near(b, way, way)

    for b in range(3):
        grams(b, b + 1)
        far(b)
    grams(4, 6)
    plain(0)
    grams(3, 4)
    grams(6, 10)
    joined(0)
    far(3)
    plain(1)
    grams(10, 16)
    joined(1)
    plain(2)
    joined(2)
    plain(3)
    joined(3)

    def arrived(b):
        for slot in (b, 4 + b):
            for h, rows in enumerate(halves):
                copy(r2.at[slot, rows], r2.at[slot, rows], R2 + 2 * slot + h, partner).wait_recv()
        part[12 + b] = part[12 + b] + r2[b] + r2[4 + b]

    def wait_query(i, carry):
        copy(qstage.at[i], qrx.at[i], QRY + i, partner).wait_recv()
        return carry

    lax.fori_loop(1, CHIPS, wait_query, 0)
    for lb in range(4):
        cond[core, chip, :, lb * LANES : (lb + 1) * LANES] = jnp.concatenate(
            [qrx[i, lb * 4 : lb * 4 + 4, :] for i in range(CHIPS)], axis=0
        )

    second_to = (dev(fst, snd + 1), dev(fst, snd - 1))
    arrived(0)
    over = []
    for way, rows in enumerate(halves):
        over.append(copy(part.at[12, rows], r3.at[rows], R3 + way, second_to[way]))
        over[-1].start()
    onto = []
    for way, rows in enumerate(halves):
        arrived(1 + way)
        over[way].wait_recv()
        part[13 + way, rows] = part[13 + way, rows] + r3[rows]
        onto.append(copy(part.at[13 + way], r4.at[way], R4 + way, second_to[way]))
        onto[-1].start()
    arrived(3)
    for c in onto:
        c.wait_recv()
    half[core] = (part[15] + r4[0] + r4[1]) * (1.0 / total_rows)
    exchange = copy(half.at[core], half.at[core], EXC, partner)
    exchange.start()

    copy(half.at[1 - core], half.at[1 - core], EXC, partner).wait_recv()

    def block_at(a, b):
        return pl.ds(a * LANES, LANES), pl.ds(b * LANES, LANES)

    squares = jnp.zeros((LANES, LANES), F32)
    traces = jnp.zeros((LANES, LANES), F32)
    diagonals = {}
    for h in range(2):
        b0, b1, b2, b3 = [(i + h) % 4 for i in range(4)]
        packed = half[h, 0:128, :]
        packed_t = packed.T
        spare = jnp.broadcast_to(half[h, 512:513, :], (LANES, LANES))
        diagonals[b0] = jnp.where(upper, packed, packed_t)
        diagonals[b2] = jnp.where(eye, spare, jnp.where(upper, packed_t, packed))
        for start, a, b in ((128, b0, b1), (256, b2, b3), (384, b0, b2)):
            block = half[h, start : start + LANES, :]
            squares = squares + 2.0 * (block * block)
            p_ref[block_at(a, b)] = block
            p_ref[block_at(b, a)] = block.T
    for block in diagonals.values():
        traces = traces + jnp.where(eye, block, 0.0)
    shift = damp_ref[chip] * jnp.sum(traces) / WIDTH
    for a, block in diagonals.items():
        block = block + jnp.where(eye, shift, 0.0)
        squares = squares + block * block
        p_ref[block_at(a, a)] = block
    scaled = jnp.full((8, LANES), jnp.sum(squares) + EPSILON, F32)
    unit = (1.0 / jnp.sqrt(scaled))[0:1, 0:1]
    p_ref[...] = p_ref[...] * unit
    cond[core, chip] = cond[core, chip] * unit

    def twice(a_high, a_low, b_high, b_low):
        both = dot(jnp.concatenate([a_high, a_low], axis=0), b_high)
        rows = a_high.shape[0]
        return both[:rows] + (both[rows:] + dot(a_high, b_low))

    def newton(step, carry):
        value = p_ref[...]
        vector = cond[core, chip]
        high, low_ = split(value)
        v_high, v_low = split(vector)
        left_hi = jnp.concatenate([high[:MID], v_high], axis=0)
        left_lo = jnp.concatenate([low_[:MID], v_low], axis=0)
        prod = twice(left_hi, left_lo, high, low_)
        corner = twice(high[MID:], low_[MID:], high[:, MID:], low_[:, MID:])
        upper_rows = 2.0 * value[:MID] - prod[:MID]
        p_ref[:MID, :] = upper_rows
        p_ref[MID:, :MID] = upper_rows[:, MID:].T
        p_ref[MID:, MID:] = 2.0 * value[MID:, MID:] - corner
        cond[core, chip] = 2.0 * vector - prod[MID:]
        return carry

    for step in range(NEWTON_STEPS - 2):
        newton(step, 0)
    high, low_ = split(p_ref[...])

    def apply(vector):
        v_high, v_low = split(vector)
        return twice(v_high, v_low, high, low_)

    vector = cond[core, chip]
    vector = 2.0 * vector - apply(vector)
    once = apply(vector)
    vector = 2.0 * vector - (2.0 * once - apply(once))
    cond[core, chip] = vector

    halves = (pl.ds(0, HALF_Q // 2), pl.ds(HALF_Q // 2, HALF_Q // 2))

    def at(a, b, rows=None):
        ref = cond.at[core, chip_at(wrap(fst + a), wrap(snd + b))]
        return ref if rows is None else ref.at[rows]

    def go(ref, place, device):
        c = copy(ref, ref, place, device)
        c.start()
        sent.append(c)

    def come(ref, place):
        copy(ref, ref, place, partner).wait_recv()

    def hand_over(a, b):
        go(at(a, b), PAR + a * 4 + b, partner)

    def both_ways(a, b, place, devices):
        for n in range(2):
            for way in range(2):
                h = n ^ way
                go(at(a, b, halves[h]), place + 2 * way + n, devices[way])

    def along_first(b):
        both_ways(0, b, FST + 6 * b, first_to)

    def pass_first(b):
        for way in range(2):
            come(at(3 - 2 * way, b, halves[way]), FST + 6 * b + 2 * way)
            go(at(3 - 2 * way, b, halves[way]), FST + 6 * b + 4 + way, first_to[way])

    def rest_first(b):
        for way in range(2):
            come(at(3 - 2 * way, b, halves[1 - way]), FST + 6 * b + 2 * way + 1)
            hand_over(3 - 2 * way, b)

    def far_first(b):
        for way in range(2):
            come(at(2, b, halves[way]), FST + 6 * b + 4 + way)
            go(at(2, b, halves[way]), PAR_LOW + b if way else PAR + 8 + b, partner)

    def score(c, j):
        left = jnp.concatenate(split(cond[c, j]), axis=0)
        got = dot_t(left, grads[j])
        got = got[:, :ROWS] + got[:, ROWS:]
        rows = pl.ds(pl.multiple_of(c * HALF_Q, HALF_Q), HALF_Q)
        acc[rows, :] = acc[rows, :] + (got[:HALF_Q] + got[HALF_Q:])

    def own(a, b):
        score(core, chip_at(wrap(fst + a), wrap(snd + b)))

    def other(a, b):
        c = 1 - core
        j = chip_at(wrap(snd + a), wrap(fst + b), c)
        if a == 2:
            come(cond.at[c, j, halves[0]], PAR + 8 + b)
            come(cond.at[c, j, halves[1]], PAR_LOW + b)
        else:
            come(cond.at[c, j], PAR + a * 4 + b)
        score(c, j)

    acc[...] = jnp.zeros((2 * HALF_Q, ROWS), F32)
    both_ways(0, 0, SEC, second_to)
    along_first(0)
    hand_over(0, 0)
    for way in range(2):
        come(at(0, 3 - 2 * way, halves[way]), SEC + 2 * way)
        go(at(0, 3 - 2 * way, halves[way]), SEC + 4 + way, second_to[way])
    pass_first(0)
    for way in range(2):
        come(at(0, 3 - 2 * way, halves[1 - way]), SEC + 2 * way + 1)
        along_first(3 - 2 * way)
        hand_over(0, 3 - 2 * way)
    rest_first(0)
    own(0, 0)
    for way in range(2):
        come(at(0, 2, halves[way]), SEC + 4 + way)
    along_first(2)
    hand_over(0, 2)
    own(0, 3)
    own(0, 1)
    other(0, 0)
    pass_first(3)
    rest_first(3)
    own(0, 2)
    own(3, 0)
    pass_first(1)
    rest_first(1)
    own(1, 0)
    other(0, 3)
    far_first(0)
    other(0, 1)
    pass_first(2)
    rest_first(2)
    own(3, 3)
    own(1, 3)
    other(3, 0)
    other(1, 0)
    far_first(3)
    own(3, 1)
    own(1, 1)
    other(0, 2)
    far_first(1)
    own(2, 0)
    for a, b in ((3, 2), (1, 2), (2, 3)):
        own(a, b)
    for a, b in ((3, 3), (1, 3), (3, 1)):
        other(a, b)
    far_first(2)
    own(2, 1)
    other(1, 1)
    other(2, 0)
    own(2, 2)
    for a, b in ((3, 2), (1, 2), (2, 3), (2, 1), (2, 2)):
        other(a, b)

    done = acc[...] * scale
    for h in range(2):
        zout[:, 8 * h : 8 * h + 8, :] = done[h * HALF_Q : (h + 1) * HALF_Q].reshape(DEPTH, 8, ROWS)

    def send_scores(i, carry):
        there = lax.rem(z + i, DEPTH)
        copy(zout.at[there], zin.at[i], ZED + i, (there, dp)).start()
        return carry

    lax.fori_loop(DEPTH // 2, DEPTH, send_scores, 0)
    lax.fori_loop(1, DEPTH // 2, send_scores, 0)
    def sent_raw(k, carry):
        copy(stage.at[0], rx.at[0], RAW + k, partner).wait_send()
        return carry

    lax.fori_loop(0, CHIPS, sent_raw, 0)

    def sent_query(i, carry):
        copy(qstage.at[0], qrx.at[0], QRY + i, partner).wait_send()
        return carry

    lax.fori_loop(1, CHIPS, sent_query, 0)

    for c in (*over, *onto, exchange, *sent):
        c.wait_send()

    total = zout[z]
    for i in range(1, DEPTH):
        copy(zin.at[i], zin.at[i], ZED + i, partner).wait_recv()
        total = total + zin[i]
    out_ref[...] = jnp.concatenate([total[0:4], total[8:12], total[4:8], total[12:16]], axis=0)

    def sent_scores(i, carry):
        copy(zout.at[0], zin.at[0], ZED + i, partner).wait_send()
        return carry

    lax.fori_loop(1, DEPTH, sent_scores, 0)


def per_device(train_grads, queries, damping):
    rows, modules, width = train_grads.shape
    total_rows = rows * lax.axis_size("dp")
    scale = 1.0 / math.sqrt(modules * lax.axis_size("mod") * width)
    vmem = pltpu.VMEM
    out = pl.pallas_call(
        functools.partial(kernel, total_rows, scale),
        out_shape=jax.ShapeDtypeStruct((16, ROWS), F32),
        in_specs=[
            pl.BlockSpec(memory_space=pl.ANY),
            pl.BlockSpec(memory_space=pl.ANY),
            pl.BlockSpec(memory_space=pltpu.SMEM),
        ],
        out_specs=pl.BlockSpec(memory_space=vmem),
        scratch_shapes=[
            vmem((4, ROWS * CHIPS, LANES), F32),
            vmem((4, 4 * CHIPS, LANES), F32),
            vmem((CHIPS, ROWS, WIDTH), F32),
            vmem((CHIPS, ROWS, WIDTH), F32),
            vmem((CHIPS, 16, LANES), F32),
            vmem((CHIPS, 16, LANES), F32),
            vmem((CHIPS, TRI, LANES), F32),
            vmem((4, TRI, LANES), F32),
            vmem((8, TRI, LANES), F32),
            vmem((TRI, LANES), F32),
            vmem((2, TRI, LANES), F32),
            vmem((2, TRI, LANES), F32),
            vmem((WIDTH, WIDTH), F32),
            vmem((2, CHIPS, HALF_Q, WIDTH), F32),
            vmem((CHIPS, 2 * ROWS, WIDTH), BF16),
            vmem((2 * HALF_Q, ROWS), F32),
            vmem((DEPTH, 16, ROWS), F32),
            vmem((DEPTH, 16, ROWS), F32),
            pltpu.SemaphoreType.DMA((8,)),
            pltpu.SemaphoreType.DMA((COPIES,)),
            pltpu.SemaphoreType.DMA((COPIES,)),
        ],
        compiler_params=pltpu.CompilerParams(
            collective_id=0, has_side_effects=True, vmem_limit_bytes=60 * 2**20
        ),
    )(train_grads.reshape(rows * modules, width), queries.reshape(-1, width), damping)
    return out.T


def solution(mesh):
    return jax.shard_map(
        per_device,
        mesh=mesh,
        in_specs=(P("dp", "mod", None), P("dp", "mod", None), P("mod")),
        out_specs=P("dp", "mod"),
        check_vma=False,
    )
```
